512 devices in a mesh: seq: 64 (over z_lo, y, core), head: 8 (over z_hi, x).
Axes of the slice: x: 4, y: 8, z: 8 (z_hi: 2, z_lo: 4; z = z_hi * 4 + z_lo), core: 2. Of those that a mesh axis runs over, the one named last changes fastest.
Arguments:
- queries: bfloat16 [8192, 64, 128], P('seq', 'head'), may hold values from -11 to 11
- key_heads: bfloat16 [8192, 8, 128], P('seq', 'head'), may hold values from -20 to 20
- value_heads: bfloat16 [8192, 8, 128], P('seq', 'head'), may hold values from -6 to 6
- fold_map: int32 [64], replicated, may hold values from 0 to 63, as said below
- partner_map: int32 [2, 64], replicated, may hold values from 0 to 63, as said below
- out_weight: bfloat16 [8192, 5120], P('head', 'seq'), may hold values from -0.1875 to 0.1875
Outputs:
- projected: bfloat16 [8192, 5120], P('seq', 'head')
The draws below stay inside these ranges and needn't reach their ends.
Inputs may be any that keep to these rules, and one draw needn't show every extreme that they name: `fold_map`: a permutation of 0 to 63. `partner_map`: round r pairs index i with index i XOR m_r, where m_r is nonzero and the two rounds have different m_r.
All inputs are finite; a program needn't handle non-finite values.
Results may differ from the reference program's by a relative error of at most 0.0051.
Values may be sent and summed in bfloat16 or wider, within the bound.
A program may use at most 64 MiB of HBM per device.

```python
import math
import jax
import jax.numpy as jnp
from jax import lax

HEADS = 64
KV_HEADS = 8
HEAD_DIM = 128
D = 5120
BLOCK = 64
TOKENS = 8192
N_SEQ = 64


def draw_queries(key, part):
    key = jax.random.fold_in(key, 11)
    drawn = jnp.clip(jax.random.normal(key, (TOKENS, HEADS, HEAD_DIM), jnp.float32), -6.0, 6.0)
    return drawn.astype(jnp.bfloat16)


def draw_key_heads(key, part):
    key = jax.random.fold_in(key, 12)
    key_base, key_rows, key_cols = jax.random.split(key, 3)
    row_scale = jnp.exp(jax.random.uniform(key_rows, (TOKENS, KV_HEADS, 1), jnp.float32, jnp.log(0.3), jnp.log(3.0)))
    col_scale = jnp.exp(jax.random.uniform(key_cols, (1, 1, HEAD_DIM), jnp.float32, jnp.log(0.6), jnp.log(1.6)))
    drawn = jnp.clip(jax.random.normal(key_base, (TOKENS, KV_HEADS, HEAD_DIM), jnp.float32), -4.0, 4.0) * row_scale * col_scale
    return drawn.astype(jnp.bfloat16)


def draw_fold_map(key, part):
    key = jax.random.fold_in(key, 13)
    return jax.random.permutation(key, N_SEQ).astype(jnp.int32)


def draw_partner_map(key, part):
    key = jax.random.fold_in(key, 14)
    key_first, key_step = jax.random.split(key)
    first_mask = jax.random.randint(key_first, (), 1, N_SEQ, dtype=jnp.int32)
    step_size = jax.random.randint(key_step, (), 1, N_SEQ - 1, dtype=jnp.int32)
    second_mask = 1 + (first_mask - 1 + step_size) % (N_SEQ - 1)
    round_masks = jnp.stack([first_mask, second_mask]).astype(jnp.int32)
    return jnp.bitwise_xor(jnp.arange(N_SEQ, dtype=jnp.int32)[None, :], round_masks[:, None]).astype(jnp.int32)


def with_spikes(values, own_key, source, target, shards_of, factor):
    owner, partner = [(jnp.arange(values.shape[dim]) // (values.shape[dim] // shards_of)).reshape([-1 if axis == dim else 1 for axis in range(values.ndim)]) for dim in (source, target)]
    chosen = jax.random.permutation(own_key, shards_of)[partner]
    strong = (owner == chosen) | (owner == (partner + shards_of // 2) % shards_of)
    return jnp.where(strong, factor * values, values)


def levels(rng, dims, shards, low, high):
    gain = 1.0
    for position, parts in shards:
        steps = jax.random.uniform(jax.random.fold_in(jax.random.fold_in(rng, 6), position), (parts,), jnp.float32, low / len(shards), high / len(shards))
        gain = gain * jnp.repeat(jnp.exp(steps), dims[position] // parts).reshape((-1,) + (1,) * (len(dims) - 1 - position))
    return gain


def centred(stream_key, dims, scale, most, cuts=(), kind=jnp.bfloat16):
    result = jax.random.normal(stream_key, dims, jnp.float32) * scale
    if len(cuts) > 0:
        result = levels(stream_key, dims, cuts, -0.22, 0.18) * result
    return jnp.clip(result, min=-most, max=most).astype(kind)


def bell_draw_with(own_key, dims, spread, limit, cuts, heavy, held_as=jnp.bfloat16):
    result = spread * jax.random.normal(own_key, dims, jnp.float32)
    if cuts:
        result = result * levels(own_key, dims, cuts, -0.22, 0.18)
    return jnp.clip(with_spikes(result, jax.random.fold_in(own_key, 3), *heavy), -limit, limit).astype(held_as)


def setup_inputs(seed: int = 0) -> dict:
    key_list = jax.random.split(jax.random.key(seed), 7)
    queries = draw_queries(jax.random.fold_in(key_list[6], 71), 0)
    key_heads = draw_key_heads(jax.random.fold_in(key_list[6], 71), 0)
    value_heads = centred(key_list[2], (TOKENS, KV_HEADS, HEAD_DIM), 1.0, 6.0, ((0, 64), (1, 8)))
    fold_map = draw_fold_map(jax.random.fold_in(key_list[6], 71), 0)
    partner_map = draw_partner_map(jax.random.fold_in(key_list[6], 71), 0)
    out_weight = bell_draw_with(key_list[5], (HEADS * HEAD_DIM, D), (HEADS * HEAD_DIM) ** -0.5, 0.1875, ((0, 8), (1, 64)), (0, 1, 64, 4.0))
    return {"queries": queries, "key_heads": key_heads, "value_heads": value_heads, "fold_map": fold_map, "partner_map": partner_map, "out_weight": out_weight}


def block_places(fold_map):
    offsets = jnp.arange(BLOCK, dtype=jnp.int32)
    lower_rows = fold_map[:, None] * BLOCK + offsets[None, :]
    upper_rows = (2 * N_SEQ - 1 - fold_map)[:, None] * BLOCK + offsets[None, :]
    return jnp.concatenate([lower_rows, upper_rows], axis=1).astype(jnp.int32)

def reference(queries, key_heads, value_heads, fold_map, partner_map, out_weight):
    group_size = HEADS // KV_HEADS
    places = block_places(fold_map)
    query_dev = queries.reshape(N_SEQ, 2 * BLOCK, KV_HEADS, group_size, HEAD_DIM)
    key_dev = key_heads.reshape(N_SEQ, 2 * BLOCK, KV_HEADS, HEAD_DIM)
    value_dev = value_heads.reshape(N_SEQ, 2 * BLOCK, KV_HEADS, HEAD_DIM)
    score_scale = 1.0 / math.sqrt(HEAD_DIM)

    def attend(device):
        sources = jnp.stack([device, partner_map[0, device], partner_map[1, device]]).astype(jnp.int32)
        seen_keys = key_dev[sources].reshape(6 * BLOCK, KV_HEADS, HEAD_DIM)
        seen_values = value_dev[sources].reshape(6 * BLOCK, KV_HEADS, HEAD_DIM)
        seen_places = places[sources].reshape(6 * BLOCK)
        own_places = places[device]
        visible = seen_places[None, :] <= own_places[:, None]
        scores = jnp.einsum('rhje,khe->hjrk', query_dev[device].astype(jnp.float32), seen_keys.astype(jnp.float32)) * score_scale
        scores = jnp.where(visible, scores, -jnp.inf)
        row_max = lax.optimization_barrier(jnp.max(scores, axis=-1, keepdims=True))
        weights = jnp.exp(scores - row_max)
        row_total = lax.optimization_barrier(jnp.sum(weights, axis=-1))
        rounded = weights.astype(jnp.bfloat16).astype(jnp.float32)
        summed = jnp.einsum('hjrk,khe->rhje', rounded, seen_values.astype(jnp.float32))
        attended = summed / jnp.moveaxis(row_total, 2, 0)[..., None]
        return attended.reshape(2 * BLOCK, HEADS, HEAD_DIM).astype(jnp.bfloat16)
    attended = lax.map(attend, jnp.arange(N_SEQ, dtype=jnp.int32)).reshape(TOKENS, HEADS * HEAD_DIM)
    return jnp.dot(attended, out_weight, preferred_element_type=jnp.float32).astype(jnp.bfloat16)
```

```python
import math

import jax
import jax.numpy as jnp
from jax import lax
from jax.experimental import pallas as pl
from jax.experimental.pallas import tpu as pltpu
from jax.sharding import PartitionSpec as P

MESH = pl.DeviceIdType.MESH
HEADS = 8
DIM = 128
ROWS = 128
HALF = 64
DEPTH = HEADS * DIM
CHUNK = 80
QUARTER = 320
N_Y = 8
BLOCKS = 128


def dot_nt(a, b):
    return lax.dot_general(a, b, (((1,), (1,)), ((), ())), preferred_element_type=jnp.float32)


def dot_nn(a, b):
    return lax.dot_general(a, b, (((1,), (0,)), ((), ())), preferred_element_type=jnp.float32)


def kernel(
    q_ref, k_ref, v_ref, fold_ref, partner_ref, w_ref, out_ref,
    kv_y, kv_z1, kv_z2, kv_c, q_wide, q_heads, k_all, v_all,
    w_all, att, x1_out, x1_in, x2_out, x2_in, kept, s2_out, s2_in,
    kv_send, kv_recv, w_send, w_recv, pair_send, pair_recv,
    step_send, step_recv, att_send, att_recv, x_send, x_recv, s2_send, s2_recv,
):
    seq = lax.axis_index("seq")
    head = lax.axis_index("head")
    z, y, core = seq // 16, (seq // 2) % 8, seq % 2
    z_hi, x = head // 4, head % 4

    def at(z_to, y_to, core_to):
        return z_to * 16 + y_to * 2 + core_to

    up = (at(z, (y + 1) % 8, core), head)
    down = (at(z, (y + 7) % 8, core), head)
    z_flip = [None, (seq ^ 16, head), (seq ^ 32, head)]
    other_core = (seq ^ 1, head)
    x_flip = {1: (seq, head ^ 1), 3: (seq, head ^ 3)}

    target_head = 2 * z + x // 2
    targets = [(seq ^ (16 * t), target_head) for t in range(4)]
    home = target_head == head
    source_seq = at(head // 2, y, core)

    barrier = pltpu.get_barrier_semaphore()
    for peer in (up, down, z_flip[1], z_flip[2], other_core, x_flip[1], x_flip[3]):
        pl.semaphore_signal(barrier, inc=1, device_id=peer, device_id_type=MESH)
    for hi in range(2):
        for side in range(2):
            source_head = hi * 4 + 2 * (head % 2) + side
            mine = jnp.logical_and(source_seq == seq, source_head == head)

            @pl.when(jnp.logical_not(mine))
            def _():
                pl.semaphore_signal(
                    barrier, inc=1, device_id=(source_seq, source_head), device_id_type=MESH
                )

    kv_y[0, 0:ROWS, :] = k_ref[...]
    kv_y[0, ROWS:, :] = jnp.transpose(v_ref[...].astype(jnp.float32)).astype(jnp.bfloat16)
    pl.semaphore_wait(barrier, 11 - jnp.where(home, 1, 0))

    def remote(src, dst, send, recv, peer):
        copy = pltpu.make_async_remote_copy(
            src_ref=src, dst_ref=dst, send_sem=send, recv_sem=recv,
            device_id=peer, device_id_type=MESH,
        )
        copy.start()
        return copy

    sent = []

    def kv_step(way, k):
        src_slot = k - 1 if way == 0 else (8 - (k - 1)) % 8
        dst_slot = k if way == 0 else 8 - k
        src, dst = kv_y.at[src_slot], kv_y.at[dst_slot]
        if k == 4:
            part = pl.ds(ROWS * way, ROWS)
            src, dst = kv_y.at[src_slot, part], kv_y.at[dst_slot, part]
        copy = remote(
            src, dst, kv_send.at[way, k - 1], kv_recv.at[way, k - 1], up if way == 0 else down
        )
        sent.append(copy)
        return copy

    def w_rows(k):
        return pl.multiple_of((((y - k) % 8) * 2 + core) * CHUNK, 16)

    def w_step(way, k):
        slot = k - 1 if way == 0 else (8 - (k - 1)) % 8
        first = w_rows(slot)
        rows = CHUNK
        if k == 4:
            first, rows = (first, 48) if way == 0 else (first + 48, 32)
        place = pl.ds(pl.multiple_of(first, 16), rows)
        copy = remote(
            w_all.at[place], w_all.at[place], w_send.at[way, k - 1], w_recv.at[way, k - 1],
            up if way == 0 else down,
        )
        sent.append(copy)
        return copy

    def w_pair(k):
        place = pl.ds(w_rows(k), CHUNK)
        copy = remote(
            w_all.at[place], w_all.at[place], pair_send.at[k], pair_recv.at[k], other_core
        )
        sent.append(copy)
        return copy

    kv_up, kv_down = kv_step(0, 1), kv_step(1, 1)
    w_all[pl.ds(w_rows(0), CHUNK), :] = w_ref[...]
    pairs = [w_pair(0)]
    q_wide[...] = q_ref[...].astype(jnp.float32)
    for k in range(2, 5):
        kv_up.wait_recv()
        kv_up = kv_step(0, k)
        kv_down.wait_recv()
        kv_down = kv_step(1, k)
        if k == 2:
            for h in range(HEADS):
                q_heads[pl.ds(h * ROWS, ROWS), :] = q_wide[
                    pl.ds(h, ROWS, stride=HEADS), :
                ].astype(jnp.bfloat16)
    w_up, w_down = w_step(0, 1), w_step(1, 1)
    k_all[0:ROWS, :] = k_ref[...]
    v_all[:, 0:ROWS] = kv_y[0, ROWS:, :]
    kv_up.wait_recv()
    kv_down.wait_recv()

    partners = [partner_ref[0, seq], partner_ref[1, seq]]
    flips = [partner ^ seq for partner in partners]

    for i in range(2):
        y_from = (partners[i] >> 1) & 7
        kv_z1[0, i] = kv_y[(y - y_from) & 7]
    step = remote(kv_z1.at[0], kv_z1.at[1], step_send.at[0], step_recv.at[0], z_flip[1])
    sent.append(step)

    step.wait_recv()
    for i in range(2):
        kv_z2[0, i] = kv_z1[(flips[i] >> 4) & 1, i]
    step = remote(kv_z2.at[0], kv_z2.at[1], step_send.at[1], step_recv.at[1], z_flip[2])
    sent.append(step)

    w_up.wait_recv()
    w_up = w_step(0, 2)
    w_down.wait_recv()
    w_down = w_step(1, 2)
    pairs += [w_pair(1), w_pair(7)]

    step.wait_recv()
    for i in range(2):
        kv_c[0, i] = kv_z2[(flips[i] >> 5) & 1, i]
    step = remote(kv_c.at[0], kv_c.at[1], step_send.at[2], step_recv.at[2], other_core)
    sent.append(step)

    w_up.wait_recv()
    w_up = w_step(0, 3)
    w_down.wait_recv()
    w_down = w_step(1, 3)
    pairs += [w_pair(2), w_pair(6)]

    step.wait_recv()
    for i in range(2):
        from_core = flips[i] & 1
        k_all[pl.ds((i + 1) * ROWS, ROWS), :] = kv_c[from_core, i, 0:ROWS, :]
        v_all[:, pl.ds((i + 1) * ROWS, ROWS)] = kv_c[from_core, i, ROWS:, :]

    def places(fold, offset):
        return offset + jnp.where(
            offset < HALF, fold * HALF, (BLOCKS - 1 - fold) * HALF - HALF
        )

    down_iota = lax.broadcasted_iota(jnp.int32, (ROWS, ROWS), 0)
    across_iota = lax.broadcasted_iota(jnp.int32, (ROWS, ROWS), 1)
    own_places = places(fold_ref[seq], across_iota)
    hidden = []
    for device in (seq, partners[0], partners[1]):
        seen = places(fold_ref[device], down_iota) <= own_places
        hidden.append(jnp.where(seen, 0.0, -jnp.inf).astype(jnp.float32))
    bias = jnp.concatenate(hidden, axis=0)
    bias = jnp.concatenate([bias] * 4, axis=1)
    scale = 1.0 / math.sqrt(DIM)
    att_copies = {}

    for part in range(2):
        heads = pl.ds(part * 4 * ROWS, 4 * ROWS)
        scores = dot_nt(k_all[...], q_heads[heads, :]) * scale + bias
        top = jnp.max(scores, axis=0, keepdims=True)
        weights = jnp.exp(scores - top)
        total = jnp.sum(weights, axis=0, keepdims=True)
        summed = dot_nn(v_all[...], weights.astype(jnp.bfloat16)) / total
        summed = summed.astype(jnp.bfloat16)
        for h in range(4):
            att[0, pl.ds((part * 4 + h) * DIM, DIM), :] = summed[:, h * ROWS : (h + 1) * ROWS]
        span = pl.ds(part * DEPTH // 2, DEPTH // 2)
        for t in (1, 2):
            copy = remote(
                att.at[0, span], att.at[t, span],
                att_send.at[t - 1, part], att_recv.at[t - 1, part], z_flip[t],
            )
            sent.append(copy)
            att_copies[t, part] = copy

    w_up.wait_recv()
    w_up = w_step(0, 4)
    w_down.wait_recv()
    w_down = w_step(1, 4)
    pairs += [w_pair(3), w_pair(5)]
    w_up.wait_recv()
    w_down.wait_recv()
    pairs.append(w_pair(4))
    for copy in pairs:
        copy.wait_recv()

    x1_copies, x2_copies = [], []

    def ways(t):
        return (1, 3) if t % 2 == 0 else (3, 1)

    def product(t, quarter):
        rows = pl.ds(pl.multiple_of(quarter * QUARTER, 16), QUARTER)
        return dot_nn(w_all[rows, :], att[t])

    def project(t):
        first, second = ways(t)
        x1_out[t, 0] = product(t, x ^ first).astype(jnp.bfloat16)
        x1_out[t, 1] = product(t, x ^ 2).astype(jnp.bfloat16)
        copy = remote(x1_out.at[t], x1_in.at[t], x_send.at[0, t], x_recv.at[0, t], x_flip[first])
        sent.append(copy)
        x1_copies.append(copy)
        kept[t, 1] = product(t, x ^ second)
        kept[t, 0] = product(t, x)

    def second_sum(t):
        second = ways(t)[1]
        x1_copies[t].wait_recv()
        x2_out[t] = (kept[t, 1] + x1_in[t, 1].astype(jnp.float32)).astype(jnp.bfloat16)
        copy = remote(x2_out.at[t], x2_in.at[t], x_send.at[1, t], x_recv.at[1, t], x_flip[second])
        sent.append(copy)
        x2_copies.append(copy)
        kept[t, 0] = kept[t, 0] + x1_in[t, 0].astype(jnp.float32)

    slot_side = x % 2

    def deliver(t):
        x2_copies[t].wait_recv()
        s2_out[t] = (kept[t, 0] + x2_in[t].astype(jnp.float32)).astype(jnp.bfloat16)

        def away():
            pltpu.make_async_remote_copy(
                src_ref=s2_out.at[t], dst_ref=s2_in.at[z_hi, slot_side],
                send_sem=s2_send.at[t], recv_sem=s2_recv.at[z_hi, slot_side],
                device_id=targets[t], device_id_type=MESH,
            ).start()

        if t:
            away()
        else:
            pl.when(jnp.logical_not(home))(away)

            @pl.when(home)
            def _():
                pltpu.make_async_copy(
                    s2_out.at[t], s2_in.at[z_hi, slot_side], s2_recv.at[z_hi, slot_side]
                ).start()

    def wait_att(t):
        for part in range(2):
            att_copies[t, part].wait_recv()

    project(0)
    wait_att(1)
    project(1)
    second_sum(0)
    for part in range(2):
        att_copies[2, part].wait_recv()
        span = pl.ds(part * DEPTH // 2, DEPTH // 2)
        copy = remote(
            att.at[2, span], att.at[3, span], att_send.at[2, part], att_recv.at[2, part],
            z_flip[1],
        )
        sent.append(copy)
        att_copies[3, part] = copy
    project(2)
    second_sum(1)
    deliver(0)
    second_sum(2)
    deliver(1)
    wait_att(3)
    project(3)
    deliver(2)
    second_sum(3)
    deliver(3)

    def last(t, hi, side):
        return pltpu.make_async_remote_copy(
            src_ref=s2_out.at[t], dst_ref=s2_in.at[hi, side],
            send_sem=s2_send.at[t], recv_sem=s2_recv.at[hi, side],
            device_id=targets[t], device_id_type=MESH,
        )

    for side in range(2):
        for hi in range(2):
            last(1, hi, side).wait_recv()
    both = s2_in[0].astype(jnp.float32) + s2_in[1].astype(jnp.float32)
    both = both.reshape(2 * QUARTER, ROWS)
    out_ref[...] = jnp.transpose(both).astype(jnp.bfloat16)

    for copy in sent:
        copy.wait_send()
    for t in range(1, 4):
        last(t, 0, 0).wait_send()

    @pl.when(jnp.logical_not(home))
    def _():
        last(0, 0, 0).wait_send()


def per_device(queries, key_heads, value_heads, fold_map, partner_map, out_weight):
    vmem = pl.BlockSpec(memory_space=pltpu.VMEM)
    smem = pl.BlockSpec(memory_space=pltpu.SMEM)
    bf16, f32 = jnp.bfloat16, jnp.float32
    dma = pltpu.SemaphoreType.DMA
    kv_rows = 2 * ROWS
    return pl.pallas_call(
        kernel,
        out_shape=jax.ShapeDtypeStruct((ROWS, 2 * QUARTER), bf16),
        in_specs=[vmem, vmem, vmem, smem, smem, vmem],
        out_specs=vmem,
        scratch_shapes=[
            pltpu.VMEM((N_Y, kv_rows, DIM), bf16),
            pltpu.VMEM((2, 2, kv_rows, DIM), bf16),
            pltpu.VMEM((2, 2, kv_rows, DIM), bf16),
            pltpu.VMEM((2, 2, kv_rows, DIM), bf16),
            pltpu.VMEM((DEPTH, DIM), f32),
            pltpu.VMEM((DEPTH, DIM), bf16),
            pltpu.VMEM((3 * ROWS, DIM), bf16),
            pltpu.VMEM((DIM, 3 * ROWS), bf16),
            pltpu.VMEM((16 * CHUNK, DEPTH), bf16),
            pltpu.VMEM((4, DEPTH, ROWS), bf16),
            pltpu.VMEM((4, 2, QUARTER, ROWS), bf16),
            pltpu.VMEM((4, 2, QUARTER, ROWS), bf16),
            pltpu.VMEM((4, QUARTER, ROWS), bf16),
            pltpu.VMEM((4, QUARTER, ROWS), bf16),
            pltpu.VMEM((4, 2, QUARTER, ROWS), f32),
            pltpu.VMEM((4, QUARTER, ROWS), bf16),
            pltpu.VMEM((2, 2, QUARTER, ROWS), bf16),
            dma((2, 4)), dma((2, 4)), dma((2, 4)), dma((2, 4)), dma((8,)), dma((8,)),
            dma((3,)), dma((3,)), dma((3, 2)), dma((3, 2)), dma((2, 4)), dma((2, 4)),
            dma((4,)), dma((2, 2)),
        ],
        compiler_params=pltpu.CompilerParams(
            collective_id=0, has_side_effects=True, vmem_limit_bytes=40 * 1024 * 1024
        ),
        cost_estimate=pl.CostEstimate(
            flops=1_550_000_000, bytes_accessed=1_000_000, transcendentals=400_000
        ),
    )(
        queries.reshape(ROWS * HEADS, DIM),
        key_heads.reshape(ROWS, DIM),
        value_heads.reshape(ROWS, DIM),
        fold_map,
        partner_map,
        out_weight.T,
    )


def solution(mesh):
    return jax.shard_map(
        per_device,
        mesh=mesh,
        in_specs=(
            P("seq", "head", None),
            P("seq", "head", None),
            P("seq", "head", None),
            P(),
            P(),
            P("head", "seq"),
        ),
        out_specs=P("seq", "head"),
        check_vma=False,
    )
```

```python
import math

import jax
import jax.numpy as jnp
from jax import lax
from jax.experimental import pallas as pl
from jax.experimental.pallas import tpu as pltpu
from jax.sharding import PartitionSpec as P

MESH = pl.DeviceIdType.MESH
HEADS = 8
DIM = 128
ROWS = 128
HALF = 64
DEPTH = HEADS * DIM
CHUNK = 80
QUARTER = 320
N_Y = 8
BLOCKS = 128


def dot_nt(a, b):
    return lax.dot_general(a, b, (((1,), (1,)), ((), ())), preferred_element_type=jnp.float32)


def dot_nn(a, b):
    return lax.dot_general(a, b, (((1,), (0,)), ((), ())), preferred_element_type=jnp.float32)


def kernel(
    q_hbm, k_hbm, v_hbm, fold_ref, partner_ref, w_hbm, out_ref,
    q_in, k_in, v_in, q_wide, q_all, kv_own, kv_y, kv_c, kv_z, w_all, att,
    kept, x_out, x_in, s2_out, s2_in,
    in_sem, y_send, y_recv, w_send, w_recv, pair_send, pair_recv, core_send, core_recv,
    q_send, q_recv, own_send, own_recv, z_send, z_recv, x_send, x_recv, s2_send, s2_recv,
):
    seq = lax.axis_index("seq")
    head = lax.axis_index("head")
    z, y, core = seq // 16, (seq // 2) % 8, seq % 2
    z_hi, x = head // 4, head % 4

    def at(z_to, y_to, core_to):
        return z_to * 16 + y_to * 2 + core_to

    def w_rows(k):
        return pl.multiple_of((((y - k) % 8) * 2 + core) * CHUNK, 16)

    w_own = pl.ds(w_rows(0), CHUNK)
    loads = [
        pltpu.make_async_copy(src, dst, in_sem.at[i])
        for i, (src, dst) in enumerate(
            ((k_hbm, k_in), (v_hbm, v_in), (q_hbm, q_in), (w_hbm, w_all.at[w_own]))
        )
    ]
    for load in loads:
        load.start()

    y_peer = {k: (at(z, (y + k) % 8, core), head) for k in (1, 2, 6, 7)}
    z_peer = {t: (seq ^ (16 * t), head) for t in (1, 2, 3)}
    x_peer = {d: (seq, head ^ d) for d in (1, 2, 3)}
    other_core = (seq ^ 1, head)

    target_head = 2 * z + x // 2
    targets = [(seq ^ (16 * t), target_head) for t in range(4)]
    home = target_head == head
    source_seq = at(head // 2, y, core)

    barrier = pltpu.get_barrier_semaphore()
    peers = [*y_peer.values(), *z_peer.values(), *x_peer.values(), other_core]
    for peer in peers:
        pl.semaphore_signal(barrier, inc=1, device_id=peer, device_id_type=MESH)
    for hi in range(2):
        for side in range(2):
            source_head = hi * 4 + 2 * (head % 2) + side
            mine = jnp.logical_and(source_seq == seq, source_head == head)

            @pl.when(jnp.logical_not(mine))
            def _():
                pl.semaphore_signal(
                    barrier, inc=1, device_id=(source_seq, source_head), device_id_type=MESH
                )

    loads[0].wait()
    loads[1].wait()
    kv_y[0, 0:ROWS, :] = k_in[...]
    kv_y[0, ROWS:, :] = jnp.transpose(v_in[...].astype(jnp.float32)).astype(jnp.bfloat16)
    loads[2].wait()
    q_wide[...] = q_in[...].astype(jnp.float32)
    for h in range(HEADS):
        q_all[0, pl.ds(h * ROWS, ROWS), :] = q_wide[
            pl.ds(h, ROWS, stride=HEADS), :
        ].astype(jnp.bfloat16)
    loads[3].wait()
    pl.semaphore_wait(barrier, len(peers) + 4 - jnp.where(home, 1, 0))

    sent = []

    def remote(src, dst, send, recv, peer):
        copy = pltpu.make_async_remote_copy(
            src_ref=src, dst_ref=dst, send_sem=send, recv_sem=recv,
            device_id=peer, device_id_type=MESH,
        )
        copy.start()
        sent.append(copy)
        return copy

    def kv_near(k):
        return remote(kv_y.at[0], kv_y.at[k], y_send.at[k], y_recv.at[k], y_peer[k])

    def kv_far(i, from_slot, to_slot, peer, part):
        return remote(
            kv_y.at[from_slot, part], kv_y.at[to_slot, part],
            y_send.at[i], y_recv.at[i], y_peer[peer],
        )

    def w_near(k):
        return remote(w_all.at[w_own], w_all.at[w_own], w_send.at[k], w_recv.at[k], y_peer[k])

    def w_far(i, slot, peer, first, rows):
        place = pl.ds(pl.multiple_of(w_rows(slot) + first, 16), rows)
        return remote(w_all.at[place], w_all.at[place], w_send.at[i], w_recv.at[i], y_peer[peer])

    def w_pair(k):
        place = pl.ds(w_rows(k), CHUNK)
        return remote(w_all.at[place], w_all.at[place], pair_send.at[k], pair_recv.at[k], other_core)

    kv_a = {k: kv_near(k) for k in (1, 7, 2, 6)}
    q_copy = {
        t: remote(q_all.at[0], q_all.at[t], q_send.at[t], q_recv.at[t], z_peer[t]) for t in (1, 2)
    }
    own_copy = {
        t: remote(kv_y.at[0], kv_own.at[t], own_send.at[t], own_recv.at[t], z_peer[t])
        for t in (1, 2)
    }
    kv_own[0] = kv_y[0]
    pairs = [w_pair(0)]

    lower, upper, whole = pl.ds(0, ROWS), pl.ds(ROWS, ROWS), pl.ds(0, 2 * ROWS)
    kv_a[2].wait_recv()
    kv_b = [kv_far(3, 2, 3, 1, whole), kv_far(4, 2, 4, 2, lower)]
    kv_a[6].wait_recv()
    kv_b += [kv_far(5, 6, 5, 7, whole), kv_far(0, 6, 4, 6, upper)]
    w_a = {k: w_near(k) for k in (1, 7, 2, 6)}
    kv_a[1].wait_recv()
    kv_a[7].wait_recv()
    for copy in kv_b:
        copy.wait_recv()

    partners = [partner_ref[0, seq], partner_ref[1, seq]]
    flips = [partner ^ seq for partner in partners]
    for i in range(2):
        kv_c[0, i] = kv_y[(y - (partners[i] >> 1)) & 7]
    step = remote(kv_c.at[0], kv_c.at[1], core_send.at[0], core_recv.at[0], other_core)
    step.wait_recv()
    for i in range(2):
        kv_z[0, i] = kv_c[flips[i] & 1, i]
    kv_step = [
        remote(kv_z.at[0], kv_z.at[t], z_send.at[t], z_recv.at[t], z_peer[t]) for t in (1, 2, 3)
    ]
    own_copy[2].wait_recv()
    own_copy[3] = remote(kv_own.at[2], kv_own.at[3], own_send.at[3], own_recv.at[3], z_peer[1])
    q_copy[2].wait_recv()
    q_copy[3] = remote(q_all.at[2], q_all.at[3], q_send.at[3], q_recv.at[3], z_peer[1])

    w_a[2].wait_recv()
    w_b = [w_far(3, 2, 1, 0, CHUNK), w_far(4, 2, 2, 0, 48)]
    w_a[6].wait_recv()
    w_b += [w_far(5, 6, 7, 0, CHUNK), w_far(0, 6, 6, 48, 32)]
    pairs += [w_pair(2), w_pair(6)]
    w_a[1].wait_recv()
    w_a[7].wait_recv()
    pairs += [w_pair(1), w_pair(7)]

    for copy in kv_step:
        copy.wait_recv()

    def places(fold, offset):
        return offset + jnp.where(
            offset < HALF, fold * HALF, (BLOCKS - 1 - fold) * HALF - HALF
        )

    down_iota = lax.broadcasted_iota(jnp.int32, (ROWS, ROWS), 0)
    across_iota = lax.broadcasted_iota(jnp.int32, (ROWS, ROWS), 1)
    scale = 1.0 / math.sqrt(DIM)

    def attend(t):
        if t % 2:
            q_copy[t].wait_recv()
            own_copy[t].wait_recv()
        device = seq ^ (16 * t)
        own_places = places(fold_ref[device], across_iota)
        hidden = []
        for source in (device, partner_ref[0, device], partner_ref[1, device]):
            seen = places(fold_ref[source], down_iota) <= own_places
            hidden.append(jnp.where(seen, 0.0, -jnp.inf).astype(jnp.float32))
        bias = jnp.concatenate(hidden, axis=0)
        bias = jnp.concatenate([bias] * 4, axis=1)
        blocks = [kv_own[t]]
        for i in range(2):
            blocks.append(kv_z[t ^ ((flips[i] >> 4) & 3), i])
        keys = jnp.concatenate([block[0:ROWS, :] for block in blocks], axis=0)
        values = jnp.concatenate([block[ROWS:, :] for block in blocks], axis=1)
        for part in range(2):
            scores = dot_nt(keys, q_all[t, pl.ds(part * 4 * ROWS, 4 * ROWS), :]) * scale + bias
            top = jnp.max(scores, axis=0, keepdims=True)
            weights = jnp.exp(scores - top)
            total = jnp.sum(weights, axis=0, keepdims=True)
            summed = dot_nn(values, weights.astype(jnp.bfloat16)) / total
            summed = summed.astype(jnp.bfloat16)
            for h in range(4):
                att[t, pl.ds((part * 4 + h) * DIM, DIM), :] = summed[:, h * ROWS : (h + 1) * ROWS]

    attend(0)
    for copy in w_b:
        copy.wait_recv()
    pairs += [w_pair(3), w_pair(5), w_pair(4)]
    attend(1)
    for copy in pairs:
        copy.wait_recv()

    x_copies = {}

    def product(t, quarter):
        rows = pl.ds(pl.multiple_of(quarter * QUARTER, 16), QUARTER)
        return dot_nn(w_all[rows, :], att[t])

    def project(t):
        for d in (2, 1, 3):
            x_out[t, d - 1] = product(t, x ^ d).astype(jnp.bfloat16)
            x_copies[t, d] = remote(
                x_out.at[t, d - 1], x_in.at[t, d - 1],
                x_send.at[t, d - 1], x_recv.at[t, d - 1], x_peer[d],
            )
        kept[t] = product(t, x)

    slot_side = x % 2

    def last(t, hi, side):
        return pltpu.make_async_remote_copy(
            src_ref=s2_out.at[t], dst_ref=s2_in.at[hi, side],
            send_sem=s2_send.at[t], recv_sem=s2_recv.at[hi, side],
            device_id=targets[t], device_id_type=MESH,
        )

    def deliver(t):
        total = kept[t]
        for d in (1, 3, 2):
            x_copies[t, d].wait_recv()
            total = total + x_in[t, d - 1].astype(jnp.float32)
        s2_out[t] = total.astype(jnp.bfloat16)
        if t:
            last(t, z_hi, slot_side).start()
        else:
            pl.when(jnp.logical_not(home))(lambda: last(t, z_hi, slot_side).start())

            @pl.when(home)
            def _():
                pltpu.make_async_copy(
                    s2_out.at[t], s2_in.at[z_hi, slot_side], s2_recv.at[z_hi, slot_side]
                ).start()

    project(0)
    project(1)
    attend(2)
    project(2)
    deliver(0)
    attend(3)
    project(3)
    deliver(1)
    deliver(2)
    deliver(3)

    for side in range(2):
        for hi in range(2):
            last(1, hi, side).wait_recv()
    both = s2_in[0].astype(jnp.float32) + s2_in[1].astype(jnp.float32)
    both = both.reshape(2 * QUARTER, ROWS)
    out_ref[...] = jnp.transpose(both).astype(jnp.bfloat16)

    for copy in sent:
        copy.wait_send()
    for t in range(1, 4):
        last(t, 0, 0).wait_send()

    @pl.when(jnp.logical_not(home))
    def _():
        last(0, 0, 0).wait_send()


def per_device(queries, key_heads, value_heads, fold_map, partner_map, out_weight):
    vmem = pl.BlockSpec(memory_space=pltpu.VMEM)
    anywhere = pl.BlockSpec(memory_space=pl.ANY)
    smem = pl.BlockSpec(memory_space=pltpu.SMEM)
    bf16, f32 = jnp.bfloat16, jnp.float32
    dma = pltpu.SemaphoreType.DMA
    kv_rows = 2 * ROWS
    return pl.pallas_call(
        kernel,
        out_shape=jax.ShapeDtypeStruct((ROWS, 2 * QUARTER), bf16),
        in_specs=[anywhere, anywhere, anywhere, smem, smem, anywhere],
        out_specs=vmem,
        scratch_shapes=[
            pltpu.VMEM((DEPTH, DIM), bf16),
            pltpu.VMEM((ROWS, DIM), bf16),
            pltpu.VMEM((ROWS, DIM), bf16),
            pltpu.VMEM((DEPTH, DIM), f32),
            pltpu.VMEM((4, DEPTH, DIM), bf16),
            pltpu.VMEM((4, kv_rows, DIM), bf16),
            pltpu.VMEM((N_Y, kv_rows, DIM), bf16),
            pltpu.VMEM((2, 2, kv_rows, DIM), bf16),
            pltpu.VMEM((4, 2, kv_rows, DIM), bf16),
            pltpu.VMEM((16 * CHUNK, DEPTH), bf16),
            pltpu.VMEM((4, DEPTH, ROWS), bf16),
            pltpu.VMEM((4, QUARTER, ROWS), f32),
            pltpu.VMEM((4, 3, QUARTER, ROWS), bf16),
            pltpu.VMEM((4, 3, QUARTER, ROWS), bf16),
            pltpu.VMEM((4, QUARTER, ROWS), bf16),
            pltpu.VMEM((2, 2, QUARTER, ROWS), bf16),
            dma((4,)), dma((8,)), dma((8,)), dma((8,)), dma((8,)), dma((8,)), dma((8,)),
            dma((1,)), dma((1,)), dma((4,)), dma((4,)), dma((4,)), dma((4,)),
            dma((4,)), dma((4,)), dma((4, 3)), dma((4, 3)), dma((4,)), dma((2, 2)),
        ],
        compiler_params=pltpu.CompilerParams(
            collective_id=0, has_side_effects=True, vmem_limit_bytes=56 * 1024 * 1024
        ),
        cost_estimate=pl.CostEstimate(
            flops=1_550_000_000, bytes_accessed=1_000_000, transcendentals=400_000
        ),
    )(
        queries.reshape(ROWS * HEADS, DIM),
        key_heads.reshape(ROWS, DIM),
        value_heads.reshape(ROWS, DIM),
        fold_map,
        partner_map,
        out_weight.T,
    )


def solution(mesh):
    return jax.shard_map(
        per_device,
        mesh=mesh,
        in_specs=(
            P("seq", "head", None),
            P("seq", "head", None),
            P("seq", "head", None),
            P(),
            P(),
            P("head", "seq"),
        ),
        out_specs=P("seq", "head"),
        check_vma=False,
    )
```

```python
import math

import jax
import jax.numpy as jnp
from jax import lax
from jax.experimental import pallas as pl
from jax.experimental.pallas import tpu as pltpu
from jax.sharding import PartitionSpec as P

MESH = pl.DeviceIdType.MESH
HEADS = 8
DIM = 128
ROWS = 128
HALF = 64
DEPTH = HEADS * DIM
CHUNK = 80
QUARTER = 320
N_Y = 8
BLOCKS = 128


def dot_nt(a, b):
    return lax.dot_general(a, b, (((1,), (1,)), ((), ())), preferred_element_type=jnp.float32)


def dot_nn(a, b):
    return lax.dot_general(a, b, (((1,), (0,)), ((), ())), preferred_element_type=jnp.float32)


def kernel(
    q_hbm, k_hbm, v_hbm, fold_ref, partner_ref, w_hbm, out_ref,
    q_in, k_in, v_in, q_wide, q_all, kv_own, k_y, v_y, k_c, v_c, kv_z, w_all, att,
    kept, x_out, x_in, s2_out, s2_in,
    in_sem, y_send, y_recv, w_send, w_recv, pair_send, pair_recv, core_send, core_recv,
    q_send, q_recv, own_send, own_recv, z_send, z_recv, x_send, x_recv, s2_send, s2_recv,
):
    seq = lax.axis_index("seq")
    head = lax.axis_index("head")
    z, y, core = seq // 16, (seq // 2) % 8, seq % 2
    z_hi, x = head // 4, head % 4

    def at(z_to, y_to, core_to):
        return z_to * 16 + y_to * 2 + core_to

    def w_rows(k):
        return pl.multiple_of((((y - k) % 8) * 2 + core) * CHUNK, 16)

    w_own = pl.ds(w_rows(0), CHUNK)
    loads = [
        pltpu.make_async_copy(src, dst, in_sem.at[i])
        for i, (src, dst) in enumerate(
            ((k_hbm, k_in), (v_hbm, v_in), (q_hbm, q_in), (w_hbm, w_all.at[w_own]))
        )
    ]
    for load in loads:
        load.start()

    y_peer = {k: (at(z, (y + k) % 8, core), head) for k in (1, 2, 6, 7)}
    z_peer = {t: (seq ^ (16 * t), head) for t in (1, 2, 3)}
    x_peer = {d: (seq, head ^ d) for d in (1, 2, 3)}
    other_core = (seq ^ 1, head)

    target_head = 2 * z + x // 2
    targets = [(seq ^ (16 * t), target_head) for t in range(4)]
    home = target_head == head
    source_seq = at(head // 2, y, core)

    barrier = pltpu.get_barrier_semaphore()
    peers = [*y_peer.values(), *z_peer.values(), *x_peer.values(), other_core]
    for peer in peers:
        pl.semaphore_signal(barrier, inc=1, device_id=peer, device_id_type=MESH)
    for hi in range(2):
        for side in range(2):
            source_head = hi * 4 + 2 * (head % 2) + side
            mine = jnp.logical_and(source_seq == seq, source_head == head)

            @pl.when(jnp.logical_not(mine))
            def _():
                pl.semaphore_signal(
                    barrier, inc=1, device_id=(source_seq, source_head), device_id_type=MESH
                )

    loads[0].wait()
    loads[1].wait()
    turned = jnp.transpose(v_in[...].astype(jnp.float32)).astype(jnp.bfloat16)
    kv_own[0, 0:ROWS, :] = k_in[...]
    kv_own[0, ROWS:, :] = turned
    k_y[0] = k_in[...]
    v_y[0] = turned
    loads[2].wait()
    q_wide[...] = q_in[...].astype(jnp.float32)
    for h in range(HEADS):
        q_all[0, pl.ds(h * ROWS, ROWS), :] = q_wide[
            pl.ds(h, ROWS, stride=HEADS), :
        ].astype(jnp.bfloat16)
    loads[3].wait()
    pl.semaphore_wait(barrier, len(peers) + 4 - jnp.where(home, 1, 0))

    sent = []

    def remote(src, dst, send, recv, peer):
        copy = pltpu.make_async_remote_copy(
            src_ref=src, dst_ref=dst, send_sem=send, recv_sem=recv,
            device_id=peer, device_id_type=MESH,
        )
        copy.start()
        sent.append(copy)
        return copy

    keys_part, values_part = pl.ds(0, ROWS), pl.ds(ROWS, ROWS)
    by_y, by_core = (k_y, v_y), (k_c, v_c)

    def kv_copy(kind, i, from_slot, to_slot, peer):
        return remote(
            by_y[kind].at[from_slot], by_y[kind].at[to_slot],
            y_send.at[kind, i], y_recv.at[kind, i], y_peer[peer],
        )

    def w_hop(k):
        copies = []
        for way, slot, peer in ((0, k - 1, 1), (1, (9 - k) % 8, 7)):
            first, rows = (0, CHUNK) if k < 4 else ((0, 48), (48, 32))[way]
            place = pl.ds(pl.multiple_of(w_rows(slot) + first, 16), rows)
            sem = (k - 1) * 2 + way
            copies.append(remote(
                w_all.at[place], w_all.at[place], w_send.at[sem], w_recv.at[sem], y_peer[peer]
            ))
        return copies

    def w_pair(k):
        place = pl.ds(w_rows(k), CHUNK)
        return remote(w_all.at[place], w_all.at[place], pair_send.at[k], pair_recv.at[k], other_core)

    kv_a = {(kind, k): kv_copy(kind, k, 0, k, k) for kind in range(2) for k in (2, 6, 1, 7)}
    q_copy = {
        t: remote(q_all.at[0], q_all.at[t], q_send.at[t], q_recv.at[t], z_peer[t]) for t in (1, 2)
    }
    own_copy = {
        t: remote(kv_own.at[0], kv_own.at[t], own_send.at[t], own_recv.at[t], z_peer[t])
        for t in (1, 2)
    }
    pairs = [w_pair(0)]

    partners = [partner_ref[0, seq], partner_ref[1, seq]]
    flips = [partner ^ seq for partner in partners]

    def pass_on(copies):
        for copy in copies:
            copy.wait_recv()

    kv_b = [[], []]
    for kind in range(2):
        kv_a[kind, 2].wait_recv()
        kv_b[kind].append(kv_copy(kind, 3, 2, 3, 1))
        if kind == 0:
            kv_b[kind].append(kv_copy(kind, 4, 2, 4, 2))
        kv_a[kind, 6].wait_recv()
        kv_b[kind].append(kv_copy(kind, 5, 6, 5, 7))
        if kind == 1:
            kv_b[kind].append(kv_copy(kind, 4, 6, 4, 6))
    hop = w_hop(1)

    core_step = []
    for kind in range(2):
        pass_on([kv_a[kind, 1], kv_a[kind, 7], *kv_b[kind]])
        for i in range(2):
            by_core[kind][0, i] = by_y[kind][(y - (partners[i] >> 1)) & 7]
        core_step.append(remote(
            by_core[kind].at[0], by_core[kind].at[1],
            core_send.at[kind], core_recv.at[kind], other_core,
        ))
    z_step = {}
    for kind in range(2):
        core_step[kind].wait_recv()
        for i in range(2):
            kv_z[0, kind, i] = by_core[kind][flips[i] & 1, i]
        for t in (1, 2):
            z_step[t, kind] = remote(
                kv_z.at[0, kind], kv_z.at[t, kind],
                z_send.at[t, kind], z_recv.at[t, kind], z_peer[t],
            )

    pass_on(hop)
    hop = w_hop(2)
    pairs += [w_pair(1), w_pair(7)]
    pass_on(hop)
    hop = w_hop(3)
    pairs += [w_pair(2), w_pair(6)]
    for kind in range(2):
        z_step[2, kind].wait_recv()
        z_step[3, kind] = remote(
            kv_z.at[2, kind], kv_z.at[3, kind], z_send.at[3, kind], z_recv.at[3, kind], z_peer[1]
        )
    pass_on(hop)
    hop = w_hop(4)
    pairs += [w_pair(3), w_pair(5)]
    for t in (1, 3):
        for kind in range(2):
            z_step[t, kind].wait_recv()
    own_copy[2].wait_recv()
    own_copy[3] = remote(kv_own.at[2], kv_own.at[3], own_send.at[3], own_recv.at[3], z_peer[1])
    q_copy[2].wait_recv()
    q_copy[3] = remote(q_all.at[2], q_all.at[3], q_send.at[3], q_recv.at[3], z_peer[1])

    def places(fold, offset):
        return offset + jnp.where(
            offset < HALF, fold * HALF, (BLOCKS - 1 - fold) * HALF - HALF
        )

    down_iota = lax.broadcasted_iota(jnp.int32, (ROWS, ROWS), 0)
    across_iota = lax.broadcasted_iota(jnp.int32, (ROWS, ROWS), 1)
    scale = 1.0 / math.sqrt(DIM)

    def attend(t):
        if t % 2:
            q_copy[t].wait_recv()
            own_copy[t].wait_recv()
        device = seq ^ (16 * t)
        own_places = places(fold_ref[device], across_iota)
        hidden = []
        for source in (device, partner_ref[0, device], partner_ref[1, device]):
            seen = places(fold_ref[source], down_iota) <= own_places
            hidden.append(jnp.where(seen, 0.0, -jnp.inf).astype(jnp.float32))
        bias = jnp.concatenate(hidden, axis=0)
        bias = jnp.concatenate([bias] * 4, axis=1)
        slots = [t ^ ((flip >> 4) & 3) for flip in flips]
        keys = jnp.concatenate(
            [kv_own[t, keys_part, :]] + [kv_z[slots[i], 0, i] for i in range(2)], axis=0
        )
        values = jnp.concatenate(
            [kv_own[t, values_part, :]] + [kv_z[slots[i], 1, i] for i in range(2)], axis=1
        )
        for part in range(2):
            scores = dot_nt(keys, q_all[t, pl.ds(part * 4 * ROWS, 4 * ROWS), :]) * scale + bias
            top = jnp.max(scores, axis=0, keepdims=True)
            weights = jnp.exp(scores - top)
            total = jnp.sum(weights, axis=0, keepdims=True)
            summed = dot_nn(values, weights.astype(jnp.bfloat16)) / total
            summed = summed.astype(jnp.bfloat16)
            for h in range(4):
                att[t, pl.ds((part * 4 + h) * DIM, DIM), :] = summed[:, h * ROWS : (h + 1) * ROWS]

    attend(0)
    pass_on(hop)
    pairs.append(w_pair(4))
    attend(1)
    pass_on(pairs)

    x_copies = {}

    def product(t, quarter):
        rows = pl.ds(pl.multiple_of(quarter * QUARTER, 16), QUARTER)
        return dot_nn(w_all[rows, :], att[t])

    def project(t):
        for d in (2, 1, 3):
            x_out[t, d - 1] = product(t, x ^ d).astype(jnp.bfloat16)
            x_copies[t, d] = remote(
                x_out.at[t, d - 1], x_in.at[t, d - 1],
                x_send.at[t, d - 1], x_recv.at[t, d - 1], x_peer[d],
            )
        kept[t] = product(t, x)

    slot_side = x % 2

    def last(t, hi, side):
        return pltpu.make_async_remote_copy(
            src_ref=s2_out.at[t], dst_ref=s2_in.at[hi, side],
            send_sem=s2_send.at[t], recv_sem=s2_recv.at[hi, side],
            device_id=targets[t], device_id_type=MESH,
        )

    def deliver(t):
        total = kept[t]
        for d in (1, 3, 2):
            x_copies[t, d].wait_recv()
            total = total + x_in[t, d - 1].astype(jnp.float32)
        s2_out[t] = total.astype(jnp.bfloat16)
        if t:
            last(t, z_hi, slot_side).start()
        else:
            pl.when(jnp.logical_not(home))(lambda: last(t, z_hi, slot_side).start())

            @pl.when(home)
            def _():
                pltpu.make_async_copy(
                    s2_out.at[t], s2_in.at[z_hi, slot_side], s2_recv.at[z_hi, slot_side]
                ).start()

    project(0)
    project(1)
    attend(2)
    project(2)
    attend(3)
    project(3)
    deliver(0)
    deliver(1)
    deliver(2)
    deliver(3)

    for side in range(2):
        for hi in range(2):
            last(1, hi, side).wait_recv()
    both = s2_in[0].astype(jnp.float32) + s2_in[1].astype(jnp.float32)
    both = both.reshape(2 * QUARTER, ROWS)
    out_ref[...] = jnp.transpose(both).astype(jnp.bfloat16)

    for copy in sent:
        copy.wait_send()
    for t in range(1, 4):
        last(t, 0, 0).wait_send()

    @pl.when(jnp.logical_not(home))
    def _():
        last(0, 0, 0).wait_send()


def per_device(queries, key_heads, value_heads, fold_map, partner_map, out_weight):
    vmem = pl.BlockSpec(memory_space=pltpu.VMEM)
    anywhere = pl.BlockSpec(memory_space=pl.ANY)
    smem = pl.BlockSpec(memory_space=pltpu.SMEM)
    bf16, f32 = jnp.bfloat16, jnp.float32
    dma = pltpu.SemaphoreType.DMA
    kv_rows = 2 * ROWS
    return pl.pallas_call(
        kernel,
        out_shape=jax.ShapeDtypeStruct((ROWS, 2 * QUARTER), bf16),
        in_specs=[anywhere, anywhere, anywhere, smem, smem, anywhere],
        out_specs=vmem,
        scratch_shapes=[
            pltpu.VMEM((DEPTH, DIM), bf16),
            pltpu.VMEM((ROWS, DIM), bf16),
            pltpu.VMEM((ROWS, DIM), bf16),
            pltpu.VMEM((DEPTH, DIM), f32),
            pltpu.VMEM((4, DEPTH, DIM), bf16),
            pltpu.VMEM((4, kv_rows, DIM), bf16),
            pltpu.VMEM((N_Y, ROWS, DIM), bf16),
            pltpu.VMEM((N_Y, ROWS, DIM), bf16),
            pltpu.VMEM((2, 2, ROWS, DIM), bf16),
            pltpu.VMEM((2, 2, ROWS, DIM), bf16),
            pltpu.VMEM((4, 2, 2, ROWS, DIM), bf16),
            pltpu.VMEM((16 * CHUNK, DEPTH), bf16),
            pltpu.VMEM((4, DEPTH, ROWS), bf16),
            pltpu.VMEM((4, QUARTER, ROWS), f32),
            pltpu.VMEM((4, 3, QUARTER, ROWS), bf16),
            pltpu.VMEM((4, 3, QUARTER, ROWS), bf16),
            pltpu.VMEM((4, QUARTER, ROWS), bf16),
            pltpu.VMEM((2, 2, QUARTER, ROWS), bf16),
            dma((4,)), dma((2, 8)), dma((2, 8)), dma((8,)), dma((8,)), dma((8,)), dma((8,)),
            dma((2,)), dma((2,)), dma((4,)), dma((4,)), dma((4,)), dma((4,)),
            dma((4, 2)), dma((4, 2)), dma((4, 3)), dma((4, 3)), dma((4,)), dma((2, 2)),
        ],
        compiler_params=pltpu.CompilerParams(
            collective_id=0, has_side_effects=True, vmem_limit_bytes=56 * 1024 * 1024
        ),
        cost_estimate=pl.CostEstimate(
            flops=1_550_000_000, bytes_accessed=1_000_000, transcendentals=400_000
        ),
    )(
        queries.reshape(ROWS * HEADS, DIM),
        key_heads.reshape(ROWS, DIM),
        value_heads.reshape(ROWS, DIM),
        fold_map,
        partner_map,
        out_weight.T,
    )


def solution(mesh):
    return jax.shard_map(
        per_device,
        mesh=mesh,
        in_specs=(
            P("seq", "head", None),
            P("seq", "head", None),
            P("seq", "head", None),
            P(),
            P(),
            P("head", "seq"),
        ),
        out_specs=P("seq", "head"),
        check_vma=False,
    )
```

```python
import math

import jax
import jax.numpy as jnp
from jax import lax
from jax.experimental import pallas as pl
from jax.experimental.pallas import tpu as pltpu
from jax.sharding import PartitionSpec as P

MESH = pl.DeviceIdType.MESH
HEADS = 8
DIM = 128
ROWS = 128
HALF = 64
DEPTH = HEADS * DIM
CHUNK = 80
QUARTER = 320
N_Y = 8
BLOCKS = 128


def dot_nt(a, b):
    return lax.dot_general(a, b, (((1,), (1,)), ((), ())), preferred_element_type=jnp.float32)


def dot_nn(a, b):
    return lax.dot_general(a, b, (((1,), (0,)), ((), ())), preferred_element_type=jnp.float32)


def kernel(
    q_hbm, k_hbm, v_hbm, fold_ref, partner_ref, w_hbm, out_ref,
    q_in, k_in, v_in, q_wide, q_all, kv_own, k_y, v_y, k_c, v_c, kv_z, w_all, att,
    kept, x_out, x_in, s2_out, s2_in,
    in_sem, y_send, y_recv, w_send, w_recv, pair_send, pair_recv, core_send, core_recv,
    q_send, q_recv, own_send, own_recv, z_send, z_recv, x_send, x_recv, s2_send, s2_recv,
):
    seq = lax.axis_index("seq")
    head = lax.axis_index("head")
    z, y, core = seq // 16, (seq // 2) % 8, seq % 2
    z_hi, x = head // 4, head % 4

    def at(z_to, y_to, core_to):
        return z_to * 16 + y_to * 2 + core_to

    def w_rows(k):
        return pl.multiple_of((((y - k) % 8) * 2 + core) * CHUNK, 16)

    w_own = pl.ds(w_rows(0), CHUNK)
    loads = [
        pltpu.make_async_copy(src, dst, in_sem.at[i])
        for i, (src, dst) in enumerate(
            ((k_hbm, k_in), (v_hbm, v_in), (q_hbm, q_in), (w_hbm, w_all.at[w_own]))
        )
    ]
    for load in loads:
        load.start()

    y_peer = {k: (at(z, (y + k) % 8, core), head) for k in (1, 2, 6, 7)}
    z_peer = {t: (seq ^ (16 * t), head) for t in (1, 2, 3)}
    x_peer = {d: (seq, head ^ d) for d in (1, 2, 3)}
    other_core = (seq ^ 1, head)

    def quarter_of(owner):
        turned = (owner + 2 * (z % 2)) % 4
        return jnp.where(turned < 2, 2 * turned, 7 - 2 * turned)

    own_quarter = quarter_of(x)
    target_head = 2 * z + own_quarter // 2
    targets = [(seq ^ (16 * t), target_head) for t in range(4)]
    home = target_head == head
    source_seq = at(head // 2, y, core)

    barrier = pltpu.get_barrier_semaphore()
    peers = [*y_peer.values(), *z_peer.values(), *x_peer.values(), other_core]
    for peer in peers:
        pl.semaphore_signal(barrier, inc=1, device_id=peer, device_id_type=MESH)
    for hi in range(2):
        for side in range(2):
            source_x = (head % 2 if side == 0 else 3 - head % 2) + 2 * ((head // 2) % 2)
            source_head = hi * 4 + source_x % 4
            mine = jnp.logical_and(source_seq == seq, source_head == head)

            @pl.when(jnp.logical_not(mine))
            def _():
                pl.semaphore_signal(
                    barrier, inc=1, device_id=(source_seq, source_head), device_id_type=MESH
                )

    loads[0].wait()
    loads[1].wait()
    turned = jnp.transpose(v_in[...].astype(jnp.float32)).astype(jnp.bfloat16)
    kv_own[0, 0:ROWS, :] = k_in[...]
    kv_own[0, ROWS:, :] = turned
    k_y[0] = k_in[...]
    v_y[0] = turned
    loads[2].wait()
    q_wide[...] = q_in[...].astype(jnp.float32)
    for h in range(HEADS):
        q_all[0, pl.ds(h * ROWS, ROWS), :] = q_wide[
            pl.ds(h, ROWS, stride=HEADS), :
        ].astype(jnp.bfloat16)
    loads[3].wait()
    pl.semaphore_wait(barrier, len(peers) + 4 - jnp.where(home, 1, 0))

    sent = []

    def remote(src, dst, send, recv, peer):
        copy = pltpu.make_async_remote_copy(
            src_ref=src, dst_ref=dst, send_sem=send, recv_sem=recv,
            device_id=peer, device_id_type=MESH,
        )
        copy.start()
        sent.append(copy)
        return copy

    keys_part, values_part = pl.ds(0, ROWS), pl.ds(ROWS, ROWS)
    by_y, by_core = (k_y, v_y), (k_c, v_c)

    def kv_copy(kind, i, from_slot, to_slot, peer):
        return remote(
            by_y[kind].at[from_slot], by_y[kind].at[to_slot],
            y_send.at[kind, i], y_recv.at[kind, i], y_peer[peer],
        )

    def w_hop(k):
        copies = []
        for way, slot, peer in ((0, k - 1, 1), (1, (9 - k) % 8, 7)):
            first, rows = (0, CHUNK) if k < 4 else ((0, 48), (48, 32))[way]
            place = pl.ds(pl.multiple_of(w_rows(slot) + first, 16), rows)
            sem = (k - 1) * 2 + way
            copies.append(remote(
                w_all.at[place], w_all.at[place], w_send.at[sem], w_recv.at[sem], y_peer[peer]
            ))
        return copies

    def w_pair(k):
        place = pl.ds(w_rows(k), CHUNK)
        return remote(w_all.at[place], w_all.at[place], pair_send.at[k], pair_recv.at[k], other_core)

    kv_a = {(kind, k): kv_copy(kind, k, 0, k, k) for kind in range(2) for k in (2, 6, 1, 7)}
    q_copy = {
        t: remote(q_all.at[0], q_all.at[t], q_send.at[t], q_recv.at[t], z_peer[t]) for t in (1, 2)
    }
    own_copy = {
        t: remote(kv_own.at[0], kv_own.at[t], own_send.at[t], own_recv.at[t], z_peer[t])
        for t in (1, 2)
    }
    pairs = [w_pair(0)]

    partners = [partner_ref[0, seq], partner_ref[1, seq]]
    flips = [partner ^ seq for partner in partners]

    def pass_on(copies):
        for copy in copies:
            copy.wait_recv()

    kv_b = [[], []]
    for kind in range(2):
        kv_a[kind, 2].wait_recv()
        kv_b[kind].append(kv_copy(kind, 3, 2, 3, 1))
        if kind == 0:
            kv_b[kind].append(kv_copy(kind, 4, 2, 4, 2))
        kv_a[kind, 6].wait_recv()
        kv_b[kind].append(kv_copy(kind, 5, 6, 5, 7))
        if kind == 1:
            kv_b[kind].append(kv_copy(kind, 4, 6, 4, 6))
    hop = w_hop(1)

    core_step = []
    for kind in range(2):
        pass_on([kv_a[kind, 1], kv_a[kind, 7], *kv_b[kind]])
        for i in range(2):
            by_core[kind][0, i] = by_y[kind][(y - (partners[i] >> 1)) & 7]
        core_step.append(remote(
            by_core[kind].at[0], by_core[kind].at[1],
            core_send.at[kind], core_recv.at[kind], other_core,
        ))
    z_step = {}
    for kind in range(2):
        core_step[kind].wait_recv()
        for i in range(2):
            kv_z[0, kind, i] = by_core[kind][flips[i] & 1, i]
        for t in (1, 2):
            z_step[t, kind] = remote(
                kv_z.at[0, kind], kv_z.at[t, kind],
                z_send.at[t, kind], z_recv.at[t, kind], z_peer[t],
            )

    pass_on(hop)
    hop = w_hop(2)
    pairs += [w_pair(1), w_pair(7)]
    pass_on(hop)
    hop = w_hop(3)
    pairs += [w_pair(2), w_pair(6)]
    for kind in range(2):
        z_step[2, kind].wait_recv()
        z_step[3, kind] = remote(
            kv_z.at[2, kind], kv_z.at[3, kind], z_send.at[3, kind], z_recv.at[3, kind], z_peer[1]
        )
    pass_on(hop)
    hop = w_hop(4)
    pairs += [w_pair(3), w_pair(5)]
    for t in (1, 3):
        for kind in range(2):
            z_step[t, kind].wait_recv()
    own_copy[2].wait_recv()
    own_copy[3] = remote(kv_own.at[2], kv_own.at[3], own_send.at[3], own_recv.at[3], z_peer[1])
    q_copy[2].wait_recv()
    q_copy[3] = remote(q_all.at[2], q_all.at[3], q_send.at[3], q_recv.at[3], z_peer[1])

    def places(fold, offset):
        return offset + jnp.where(
            offset < HALF, fold * HALF, (BLOCKS - 1 - fold) * HALF - HALF
        )

    down_iota = lax.broadcasted_iota(jnp.int32, (ROWS, ROWS), 0)
    across_iota = lax.broadcasted_iota(jnp.int32, (ROWS, ROWS), 1)
    scale = 1.0 / math.sqrt(DIM)

    def attend(t):
        if t % 2:
            q_copy[t].wait_recv()
            own_copy[t].wait_recv()
        device = seq ^ (16 * t)
        own_places = places(fold_ref[device], across_iota)
        hidden = []
        for source in (device, partner_ref[0, device], partner_ref[1, device]):
            seen = places(fold_ref[source], down_iota) <= own_places
            hidden.append(jnp.where(seen, 0.0, -jnp.inf).astype(jnp.float32))
        bias = jnp.concatenate(hidden, axis=0)
        bias = jnp.concatenate([bias] * 4, axis=1)
        slots = [t ^ ((flip >> 4) & 3) for flip in flips]
        keys = jnp.concatenate(
            [kv_own[t, keys_part, :]] + [kv_z[slots[i], 0, i] for i in range(2)], axis=0
        )
        values = jnp.concatenate(
            [kv_own[t, values_part, :]] + [kv_z[slots[i], 1, i] for i in range(2)], axis=1
        )
        for part in range(2):
            scores = dot_nt(keys, q_all[t, pl.ds(part * 4 * ROWS, 4 * ROWS), :]) * scale + bias
            top = jnp.max(scores, axis=0, keepdims=True)
            weights = jnp.exp(scores - top)
            total = jnp.sum(weights, axis=0, keepdims=True)
            summed = dot_nn(values, weights.astype(jnp.bfloat16)) / total
            summed = summed.astype(jnp.bfloat16)
            for h in range(4):
                att[t, pl.ds((part * 4 + h) * DIM, DIM), :] = summed[:, h * ROWS : (h + 1) * ROWS]

    attend(0)
    pass_on(hop)
    pairs.append(w_pair(4))
    pass_on(pairs)

    x_copies = {}

    def product(t, quarter):
        rows = pl.ds(pl.multiple_of(quarter * QUARTER, 16), QUARTER)
        return dot_nn(w_all[rows, :], att[t])

    def project(t):
        for d in (2, 1, 3):
            x_out[t, d - 1] = product(t, quarter_of(x ^ d)).astype(jnp.bfloat16)
            x_copies[t, d] = remote(
                x_out.at[t, d - 1], x_in.at[t, d - 1],
                x_send.at[t, d - 1], x_recv.at[t, d - 1], x_peer[d],
            )
        kept[t] = product(t, own_quarter)

    slot_side = own_quarter % 2

    def last(t, hi, side):
        return pltpu.make_async_remote_copy(
            src_ref=s2_out.at[t], dst_ref=s2_in.at[hi, side],
            send_sem=s2_send.at[t], recv_sem=s2_recv.at[hi, side],
            device_id=targets[t], device_id_type=MESH,
        )

    def deliver(t):
        total = kept[t]
        for d in (1, 3, 2):
            x_copies[t, d].wait_recv()
            total = total + x_in[t, d - 1].astype(jnp.float32)
        s2_out[t] = total.astype(jnp.bfloat16)
        if t:
            last(t, z_hi, slot_side).start()
        else:
            pl.when(jnp.logical_not(home))(lambda: last(t, z_hi, slot_side).start())

            @pl.when(home)
            def _():
                pltpu.make_async_copy(
                    s2_out.at[t], s2_in.at[z_hi, slot_side], s2_recv.at[z_hi, slot_side]
                ).start()

    project(0)
    attend(1)
    project(1)
    attend(2)
    project(2)
    attend(3)
    project(3)
    deliver(0)
    deliver(1)
    deliver(2)
    deliver(3)

    for side in range(2):
        for hi in range(2):
            last(1, hi, side).wait_recv()
    both = s2_in[0].astype(jnp.float32) + s2_in[1].astype(jnp.float32)
    both = both.reshape(2 * QUARTER, ROWS)
    out_ref[...] = jnp.transpose(both).astype(jnp.bfloat16)

    for copy in sent:
        copy.wait_send()
    for t in range(1, 4):
        last(t, 0, 0).wait_send()

    @pl.when(jnp.logical_not(home))
    def _():
        last(0, 0, 0).wait_send()


def per_device(queries, key_heads, value_heads, fold_map, partner_map, out_weight):
    vmem = pl.BlockSpec(memory_space=pltpu.VMEM)
    anywhere = pl.BlockSpec(memory_space=pl.ANY)
    smem = pl.BlockSpec(memory_space=pltpu.SMEM)
    bf16, f32 = jnp.bfloat16, jnp.float32
    dma = pltpu.SemaphoreType.DMA
    kv_rows = 2 * ROWS
    return pl.pallas_call(
        kernel,
        out_shape=jax.ShapeDtypeStruct((ROWS, 2 * QUARTER), bf16),
        in_specs=[anywhere, anywhere, anywhere, smem, smem, anywhere],
        out_specs=vmem,
        scratch_shapes=[
            pltpu.VMEM((DEPTH, DIM), bf16),
            pltpu.VMEM((ROWS, DIM), bf16),
            pltpu.VMEM((ROWS, DIM), bf16),
            pltpu.VMEM((DEPTH, DIM), f32),
            pltpu.VMEM((4, DEPTH, DIM), bf16),
            pltpu.VMEM((4, kv_rows, DIM), bf16),
            pltpu.VMEM((N_Y, ROWS, DIM), bf16),
            pltpu.VMEM((N_Y, ROWS, DIM), bf16),
            pltpu.VMEM((2, 2, ROWS, DIM), bf16),
            pltpu.VMEM((2, 2, ROWS, DIM), bf16),
            pltpu.VMEM((4, 2, 2, ROWS, DIM), bf16),
            pltpu.VMEM((16 * CHUNK, DEPTH), bf16),
            pltpu.VMEM((4, DEPTH, ROWS), bf16),
            pltpu.VMEM((4, QUARTER, ROWS), f32),
            pltpu.VMEM((4, 3, QUARTER, ROWS), bf16),
            pltpu.VMEM((4, 3, QUARTER, ROWS), bf16),
            pltpu.VMEM((4, QUARTER, ROWS), bf16),
            pltpu.VMEM((2, 2, QUARTER, ROWS), bf16),
            dma((4,)), dma((2, 8)), dma((2, 8)), dma((8,)), dma((8,)), dma((8,)), dma((8,)),
            dma((2,)), dma((2,)), dma((4,)), dma((4,)), dma((4,)), dma((4,)),
            dma((4, 2)), dma((4, 2)), dma((4, 3)), dma((4, 3)), dma((4,)), dma((2, 2)),
        ],
        compiler_params=pltpu.CompilerParams(
            collective_id=0, has_side_effects=True, vmem_limit_bytes=56 * 1024 * 1024
        ),
        cost_estimate=pl.CostEstimate(
            flops=1_550_000_000, bytes_accessed=1_000_000, transcendentals=400_000
        ),
    )(
        queries.reshape(ROWS * HEADS, DIM),
        key_heads.reshape(ROWS, DIM),
        value_heads.reshape(ROWS, DIM),
        fold_map,
        partner_map,
        out_weight.T,
    )


def solution(mesh):
    return jax.shard_map(
        per_device,
        mesh=mesh,
        in_specs=(
            P("seq", "head", None),
            P("seq", "head", None),
            P("seq", "head", None),
            P(),
            P(),
            P("head", "seq"),
        ),
        out_specs=P("seq", "head"),
        check_vma=False,
    )
```

```python
import math

import jax
import jax.numpy as jnp
from jax import lax
from jax.experimental import pallas as pl
from jax.experimental.pallas import tpu as pltpu
from jax.sharding import PartitionSpec as P

MESH = pl.DeviceIdType.MESH
HEADS = 8
DIM = 128
ROWS = 128
HALF = 64
DEPTH = HEADS * DIM
CHUNK = 80
QUARTER = 320
N_Y = 8
BLOCKS = 128


def dot_nt(a, b):
    return lax.dot_general(a, b, (((1,), (1,)), ((), ())), preferred_element_type=jnp.float32)


def dot_nn(a, b):
    return lax.dot_general(a, b, (((1,), (0,)), ((), ())), preferred_element_type=jnp.float32)


def kernel(
    q_hbm, k_hbm, v_hbm, fold_ref, partner_ref, w_hbm, out_ref,
    q_in, k_in, v_in, q_wide, q_all, kv_own, k_y, v_y, k_c, v_c, kv_z, w_all, att,
    kept, x_out, x_in, s2_out, s2_in,
    in_sem, y_send, y_recv, w_send, w_recv, pair_send, pair_recv, core_send, core_recv,
    q_send, q_recv, own_send, own_recv, z_send, z_recv, x_send, x_recv, s2_send, s2_recv,
):
    seq = lax.axis_index("seq")
    head = lax.axis_index("head")
    z, y, core = seq // 16, (seq // 2) % 8, seq % 2
    z_hi, x = head // 4, head % 4

    def at(z_to, y_to, core_to):
        return z_to * 16 + y_to * 2 + core_to

    def w_rows(k):
        return pl.multiple_of((((y - k) % 8) * 2 + core) * CHUNK, 16)

    w_own = pl.ds(w_rows(0), CHUNK)
    loads = [
        pltpu.make_async_copy(src, dst, in_sem.at[i])
        for i, (src, dst) in enumerate(
            ((k_hbm, k_in), (v_hbm, v_in), (q_hbm, q_in), (w_hbm, w_all.at[w_own]))
        )
    ]
    for load in loads:
        load.start()

    y_peer = {k: (at(z, (y + k) % 8, core), head) for k in (1, 2, 6, 7)}
    z_peer = {t: (seq ^ (16 * t), head) for t in (1, 2, 3)}
    x_peer = {d: (seq, head ^ d) for d in (1, 2, 3)}
    other_core = (seq ^ 1, head)

    def quarter_of(owner):
        turned = (owner + 2 * (z % 2)) % 4
        return jnp.where(turned < 2, 2 * turned, 7 - 2 * turned)

    own_quarter = quarter_of(x)
    target_head = 2 * z + own_quarter // 2
    targets = [(seq ^ (16 * t), target_head) for t in range(4)]
    home = target_head == head
    source_seq = at(head // 2, y, core)

    barrier = pltpu.get_barrier_semaphore()
    peers = [*y_peer.values(), *z_peer.values(), *x_peer.values(), other_core]
    for peer in peers:
        pl.semaphore_signal(barrier, inc=1, device_id=peer, device_id_type=MESH)
    for hi in range(2):
        for side in range(2):
            source_x = (head % 2 if side == 0 else 3 - head % 2) + 2 * ((head // 2) % 2)
            source_head = hi * 4 + source_x % 4
            mine = jnp.logical_and(source_seq == seq, source_head == head)

            @pl.when(jnp.logical_not(mine))
            def _():
                pl.semaphore_signal(
                    barrier, inc=1, device_id=(source_seq, source_head), device_id_type=MESH
                )

    loads[0].wait()
    loads[1].wait()
    turned = jnp.transpose(v_in[...].astype(jnp.float32)).astype(jnp.bfloat16)
    kv_own[0, 0:ROWS, :] = k_in[...]
    kv_own[0, ROWS:, :] = turned
    k_y[0] = k_in[...]
    v_y[0] = turned
    loads[2].wait()
    q_wide[...] = q_in[...].astype(jnp.float32)
    for h in range(HEADS):
        q_all[0, pl.ds(h * ROWS, ROWS), :] = q_wide[
            pl.ds(h, ROWS, stride=HEADS), :
        ].astype(jnp.bfloat16)
    loads[3].wait()
    pl.semaphore_wait(barrier, len(peers) + 4 - jnp.where(home, 1, 0))

    sent = []

    def remote(src, dst, send, recv, peer):
        copy = pltpu.make_async_remote_copy(
            src_ref=src, dst_ref=dst, send_sem=send, recv_sem=recv,
            device_id=peer, device_id_type=MESH,
        )
        copy.start()
        sent.append(copy)
        return copy

    def pass_on(copies):
        for copy in copies:
            copy.wait_recv()

    keys_part, values_part = pl.ds(0, ROWS), pl.ds(ROWS, ROWS)
    by_y, by_core = (k_y, v_y), (k_c, v_c)

    def kv_copy(kind, i, from_slot, to_slot, peer):
        return remote(
            by_y[kind].at[from_slot], by_y[kind].at[to_slot],
            y_send.at[kind, i], y_recv.at[kind, i], y_peer[peer],
        )

    w_streams = ((0, 48), (48, CHUNK - 48))

    def w_hop(k, stream):
        first, rows = w_streams[stream]
        copies = []
        for way, slot, peer in ((0, k - 1, 1), (1, (9 - k) % 8, 7)):
            if k == 4 and way != stream:
                continue
            place = pl.ds(pl.multiple_of(w_rows(slot) + first, 16), rows)
            sem = (k - 1, way, stream)
            copies.append(remote(
                w_all.at[place], w_all.at[place], w_send.at[sem], w_recv.at[sem], y_peer[peer]
            ))
        return copies

    hops = {}

    def w_next(k):
        for stream in range(2):
            if k > 1:
                pass_on(hops[k - 1, stream])
            if k < 5:
                hops[k, stream] = w_hop(k, stream)
        for slot in {2: (1, 7), 3: (2, 6), 4: (3, 5), 5: (4,)}.get(k, ()):
            pairs.append(w_pair(slot))

    def w_pair(k):
        place = pl.ds(w_rows(k), CHUNK)
        return remote(w_all.at[place], w_all.at[place], pair_send.at[k], pair_recv.at[k], other_core)

    kv_a = {(kind, k): kv_copy(kind, k, 0, k, k) for kind in range(2) for k in (2, 6, 1, 7)}
    q_copy = {
        t: remote(q_all.at[0], q_all.at[t], q_send.at[t], q_recv.at[t], z_peer[t]) for t in (1, 2)
    }
    own_copy = {
        t: remote(kv_own.at[0], kv_own.at[t], own_send.at[t], own_recv.at[t], z_peer[t])
        for t in (1, 2)
    }
    pairs = [w_pair(0)]

    partners = [partner_ref[0, seq], partner_ref[1, seq]]
    flips = [partner ^ seq for partner in partners]

    kv_b = [[], []]
    for kind in range(2):
        kv_a[kind, 2].wait_recv()
        kv_b[kind].append(kv_copy(kind, 3, 2, 3, 1))
        if kind == 0:
            kv_b[kind].append(kv_copy(kind, 4, 2, 4, 2))
        kv_a[kind, 6].wait_recv()
        kv_b[kind].append(kv_copy(kind, 5, 6, 5, 7))
        if kind == 1:
            kv_b[kind].append(kv_copy(kind, 4, 6, 4, 6))
    w_next(1)

    core_step = []
    for kind in range(2):
        pass_on([kv_a[kind, 1], kv_a[kind, 7], *kv_b[kind]])
        for i in range(2):
            by_core[kind][0, i] = by_y[kind][(y - (partners[i] >> 1)) & 7]
        core_step.append(remote(
            by_core[kind].at[0], by_core[kind].at[1],
            core_send.at[kind], core_recv.at[kind], other_core,
        ))
    z_step = {}
    for kind in range(2):
        core_step[kind].wait_recv()
        for i in range(2):
            kv_z[0, kind, i] = by_core[kind][flips[i] & 1, i]
        for t in (1, 2):
            z_step[t, kind] = remote(
                kv_z.at[0, kind], kv_z.at[t, kind],
                z_send.at[t, kind], z_recv.at[t, kind], z_peer[t],
            )

    w_next(2)
    w_next(3)
    for kind in range(2):
        z_step[2, kind].wait_recv()
        z_step[3, kind] = remote(
            kv_z.at[2, kind], kv_z.at[3, kind], z_send.at[3, kind], z_recv.at[3, kind], z_peer[1]
        )
    own_copy[2].wait_recv()
    own_copy[3] = remote(kv_own.at[2], kv_own.at[3], own_send.at[3], own_recv.at[3], z_peer[1])
    q_copy[2].wait_recv()
    q_copy[3] = remote(q_all.at[2], q_all.at[3], q_send.at[3], q_recv.at[3], z_peer[1])
    w_next(4)
    for t in (1, 3):
        for kind in range(2):
            z_step[t, kind].wait_recv()

    def places(fold, offset):
        return offset + jnp.where(
            offset < HALF, fold * HALF, (BLOCKS - 1 - fold) * HALF - HALF
        )

    down_iota = lax.broadcasted_iota(jnp.int32, (ROWS, ROWS), 0)
    across_iota = lax.broadcasted_iota(jnp.int32, (ROWS, ROWS), 1)
    scale = 1.0 / math.sqrt(DIM)

    def attend(t):
        if t % 2:
            q_copy[t].wait_recv()
            own_copy[t].wait_recv()
        device = seq ^ (16 * t)
        own_places = places(fold_ref[device], across_iota)
        hidden = []
        for source in (device, partner_ref[0, device], partner_ref[1, device]):
            seen = places(fold_ref[source], down_iota) <= own_places
            hidden.append(jnp.where(seen, 0.0, -jnp.inf).astype(jnp.float32))
        bias = jnp.concatenate(hidden, axis=0)
        bias = jnp.concatenate([bias] * 4, axis=1)
        slots = [t ^ ((flip >> 4) & 3) for flip in flips]
        keys = jnp.concatenate(
            [kv_own[t, keys_part, :]] + [kv_z[slots[i], 0, i] for i in range(2)], axis=0
        )
        values = jnp.concatenate(
            [kv_own[t, values_part, :]] + [kv_z[slots[i], 1, i] for i in range(2)], axis=1
        )
        for part in range(2):
            scores = dot_nt(keys, q_all[t, pl.ds(part * 4 * ROWS, 4 * ROWS), :]) * scale + bias
            top = jnp.max(scores, axis=0, keepdims=True)
            weights = jnp.exp(scores - top)
            total = jnp.sum(weights, axis=0, keepdims=True)
            summed = dot_nn(values, weights.astype(jnp.bfloat16)) / total
            summed = summed.astype(jnp.bfloat16)
            for h in range(4):
                att[t, pl.ds((part * 4 + h) * DIM, DIM), :] = summed[:, h * ROWS : (h + 1) * ROWS]

    attend(0)
    w_next(5)
    pass_on(pairs)

    x_copies = {}

    def product(t, quarter):
        rows = pl.ds(pl.multiple_of(quarter * QUARTER, 16), QUARTER)
        return dot_nn(w_all[rows, :], att[t])

    def project(t):
        for d in (2, 1, 3):
            x_out[t, d - 1] = product(t, quarter_of(x ^ d)).astype(jnp.bfloat16)
            x_copies[t, d] = remote(
                x_out.at[t, d - 1], x_in.at[t, d - 1],
                x_send.at[t, d - 1], x_recv.at[t, d - 1], x_peer[d],
            )
        kept[t] = product(t, own_quarter)

    slot_side = own_quarter % 2

    def last(t, hi, side):
        return pltpu.make_async_remote_copy(
            src_ref=s2_out.at[t], dst_ref=s2_in.at[hi, side],
            send_sem=s2_send.at[t], recv_sem=s2_recv.at[hi, side],
            device_id=targets[t], device_id_type=MESH,
        )

    def deliver(t):
        total = kept[t]
        for d in (1, 3, 2):
            x_copies[t, d].wait_recv()
            total = total + x_in[t, d - 1].astype(jnp.float32)
        s2_out[t] = total.astype(jnp.bfloat16)
        if t:
            last(t, z_hi, slot_side).start()
        else:
            pl.when(jnp.logical_not(home))(lambda: last(t, z_hi, slot_side).start())

            @pl.when(home)
            def _():
                pltpu.make_async_copy(
                    s2_out.at[t], s2_in.at[z_hi, slot_side], s2_recv.at[z_hi, slot_side]
                ).start()

    project(0)
    attend(1)
    project(1)
    attend(2)
    project(2)
    attend(3)
    project(3)
    deliver(0)
    deliver(1)
    deliver(2)
    deliver(3)

    for side in range(2):
        for hi in range(2):
            last(1, hi, side).wait_recv()
    both = s2_in[0].astype(jnp.float32) + s2_in[1].astype(jnp.float32)
    both = both.reshape(2 * QUARTER, ROWS)
    out_ref[...] = jnp.transpose(both).astype(jnp.bfloat16)

    for copy in sent:
        copy.wait_send()
    for t in range(1, 4):
        last(t, 0, 0).wait_send()

    @pl.when(jnp.logical_not(home))
    def _():
        last(0, 0, 0).wait_send()


def per_device(queries, key_heads, value_heads, fold_map, partner_map, out_weight):
    vmem = pl.BlockSpec(memory_space=pltpu.VMEM)
    anywhere = pl.BlockSpec(memory_space=pl.ANY)
    smem = pl.BlockSpec(memory_space=pltpu.SMEM)
    bf16, f32 = jnp.bfloat16, jnp.float32
    dma = pltpu.SemaphoreType.DMA
    kv_rows = 2 * ROWS
    return pl.pallas_call(
        kernel,
        out_shape=jax.ShapeDtypeStruct((ROWS, 2 * QUARTER), bf16),
        in_specs=[anywhere, anywhere, anywhere, smem, smem, anywhere],
        out_specs=vmem,
        scratch_shapes=[
            pltpu.VMEM((DEPTH, DIM), bf16),
            pltpu.VMEM((ROWS, DIM), bf16),
            pltpu.VMEM((ROWS, DIM), bf16),
            pltpu.VMEM((DEPTH, DIM), f32),
            pltpu.VMEM((4, DEPTH, DIM), bf16),
            pltpu.VMEM((4, kv_rows, DIM), bf16),
            pltpu.VMEM((N_Y, ROWS, DIM), bf16),
            pltpu.VMEM((N_Y, ROWS, DIM), bf16),
            pltpu.VMEM((2, 2, ROWS, DIM), bf16),
            pltpu.VMEM((2, 2, ROWS, DIM), bf16),
            pltpu.VMEM((4, 2, 2, ROWS, DIM), bf16),
            pltpu.VMEM((16 * CHUNK, DEPTH), bf16),
            pltpu.VMEM((4, DEPTH, ROWS), bf16),
            pltpu.VMEM((4, QUARTER, ROWS), f32),
            pltpu.VMEM((4, 3, QUARTER, ROWS), bf16),
            pltpu.VMEM((4, 3, QUARTER, ROWS), bf16),
            pltpu.VMEM((4, QUARTER, ROWS), bf16),
            pltpu.VMEM((2, 2, QUARTER, ROWS), bf16),
            dma((4,)), dma((2, 8)), dma((2, 8)), dma((4, 2, 2)), dma((4, 2, 2)), dma((8,)), dma((8,)),
            dma((2,)), dma((2,)), dma((4,)), dma((4,)), dma((4,)), dma((4,)),
            dma((4, 2)), dma((4, 2)), dma((4, 3)), dma((4, 3)), dma((4,)), dma((2, 2)),
        ],
        compiler_params=pltpu.CompilerParams(
            collective_id=0, has_side_effects=True, vmem_limit_bytes=56 * 1024 * 1024
        ),
        cost_estimate=pl.CostEstimate(
            flops=1_550_000_000, bytes_accessed=1_000_000, transcendentals=400_000
        ),
    )(
        queries.reshape(ROWS * HEADS, DIM),
        key_heads.reshape(ROWS, DIM),
        value_heads.reshape(ROWS, DIM),
        fold_map,
        partner_map,
        out_weight.T,
    )


def solution(mesh):
    return jax.shard_map(
        per_device,
        mesh=mesh,
        in_specs=(
            P("seq", "head", None),
            P("seq", "head", None),
            P("seq", "head", None),
            P(),
            P(),
            P("head", "seq"),
        ),
        out_specs=P("seq", "head"),
        check_vma=False,
    )
```

```python
import math

import jax
import jax.numpy as jnp
from jax import lax
from jax.experimental import pallas as pl
from jax.experimental.pallas import tpu as pltpu
from jax.sharding import PartitionSpec as P

MESH = pl.DeviceIdType.MESH
HEADS = 8
DIM = 128
ROWS = 128
HALF = 64
DEPTH = HEADS * DIM
CHUNK = 80
QUARTER = 320
N_Y = 8
BLOCKS = 128


def dot_nt(a, b):
    return lax.dot_general(a, b, (((1,), (1,)), ((), ())), preferred_element_type=jnp.float32)


def dot_nn(a, b):
    return lax.dot_general(a, b, (((1,), (0,)), ((), ())), preferred_element_type=jnp.float32)


def kernel(
    q_hbm, k_hbm, v_hbm, fold_ref, partner_ref, w_hbm, s2_in,
    q_in, k_in, v_in, q_wide, q_all, kv_own, k_y, v_y, k_c, v_c, kv_z, w_all, att,
    kept, x_out, x_in, s2_out,
    in_sem, y_send, y_recv, w_send, w_recv, pair_send, pair_recv, core_send, core_recv,
    q_send, q_recv, own_send, own_recv, z_send, z_recv, x_send, x_recv, s2_send, s2_recv,
):
    seq = lax.axis_index("seq")
    head = lax.axis_index("head")
    z, y, core = seq // 16, (seq // 2) % 8, seq % 2
    z_hi, x = head // 4, head % 4

    def at(z_to, y_to, core_to):
        return z_to * 16 + y_to * 2 + core_to

    def w_rows(k):
        return pl.multiple_of((((y - k) % 8) * 2 + core) * CHUNK, 16)

    w_own = pl.ds(w_rows(0), CHUNK)
    loads = [
        pltpu.make_async_copy(src, dst, in_sem.at[i])
        for i, (src, dst) in enumerate(
            ((k_hbm, k_in), (v_hbm, v_in), (q_hbm, q_in), (w_hbm, w_all.at[w_own]))
        )
    ]
    for load in loads:
        load.start()

    y_peer = {k: (at(z, (y + k) % 8, core), head) for k in (1, 2, 6, 7)}
    z_peer = {t: (seq ^ (16 * t), head) for t in (1, 2, 3)}
    x_peer = {d: (seq, head ^ d) for d in (1, 2, 3)}
    other_core = (seq ^ 1, head)

    def quarter_of(owner):
        turned = (owner + 2 * (z % 2)) % 4
        return jnp.where(turned < 2, 2 * turned, 7 - 2 * turned)

    own_quarter = quarter_of(x)
    target_head = 2 * z + own_quarter // 2
    targets = [(seq ^ (16 * t), target_head) for t in range(4)]
    home = target_head == head
    source_seq = at(head // 2, y, core)

    barrier = pltpu.get_barrier_semaphore()
    peers = [*y_peer.values(), *z_peer.values(), *x_peer.values(), other_core]
    for peer in peers:
        pl.semaphore_signal(barrier, inc=1, device_id=peer, device_id_type=MESH)
    for hi in range(2):
        for side in range(2):
            source_x = (head % 2 if side == 0 else 3 - head % 2) + 2 * ((head // 2) % 2)
            source_head = hi * 4 + source_x % 4
            mine = jnp.logical_and(source_seq == seq, source_head == head)

            @pl.when(jnp.logical_not(mine))
            def _():
                pl.semaphore_signal(
                    barrier, inc=1, device_id=(source_seq, source_head), device_id_type=MESH
                )

    loads[0].wait()
    loads[1].wait()
    turned = jnp.transpose(v_in[...].astype(jnp.float32)).astype(jnp.bfloat16)
    kv_own[0, 0:ROWS, :] = k_in[...]
    kv_own[0, ROWS:, :] = turned
    k_y[0] = k_in[...]
    v_y[0] = turned
    loads[2].wait()
    q_wide[...] = q_in[...].astype(jnp.float32)
    for h in range(HEADS):
        q_all[0, pl.ds(h * ROWS, ROWS), :] = q_wide[
            pl.ds(h, ROWS, stride=HEADS), :
        ].astype(jnp.bfloat16)
    loads[3].wait()
    pl.semaphore_wait(barrier, len(peers) + 4 - jnp.where(home, 1, 0))

    sent = []

    def remote(src, dst, send, recv, peer):
        copy = pltpu.make_async_remote_copy(
            src_ref=src, dst_ref=dst, send_sem=send, recv_sem=recv,
            device_id=peer, device_id_type=MESH,
        )
        copy.start()
        sent.append(copy)
        return copy

    def pass_on(copies):
        for copy in copies:
            copy.wait_recv()

    keys_part, values_part = pl.ds(0, ROWS), pl.ds(ROWS, ROWS)
    by_y, by_core = (k_y, v_y), (k_c, v_c)

    def kv_copy(kind, i, from_slot, to_slot, peer):
        return remote(
            by_y[kind].at[from_slot], by_y[kind].at[to_slot],
            y_send.at[kind, i], y_recv.at[kind, i], y_peer[peer],
        )

    w_streams = ((0, 48), (48, CHUNK - 48))

    def w_hop(k, stream):
        first, rows = w_streams[stream]
        copies = []
        for way, slot, peer in ((0, k - 1, 1), (1, (9 - k) % 8, 7)):
            if k == 4 and way != stream:
                continue
            place = pl.ds(pl.multiple_of(w_rows(slot) + first, 16), rows)
            sem = (k - 1, way, stream)
            copies.append(remote(
                w_all.at[place], w_all.at[place], w_send.at[sem], w_recv.at[sem], y_peer[peer]
            ))
        return copies

    hops = {}

    def w_next(k):
        for stream in range(2):
            if k > 1:
                pass_on(hops[k - 1, stream])
            if k < 5:
                hops[k, stream] = w_hop(k, stream)
        for slot in {2: (1, 7), 3: (2, 6), 4: (3, 5), 5: (4,)}.get(k, ()):
            pairs.append(w_pair(slot))

    def w_pair(k):
        place = pl.ds(w_rows(k), CHUNK)
        return remote(w_all.at[place], w_all.at[place], pair_send.at[k], pair_recv.at[k], other_core)

    kv_a = {(kind, k): kv_copy(kind, k, 0, k, k) for kind in range(2) for k in (2, 6, 1, 7)}
    q_copy = {
        t: remote(q_all.at[0], q_all.at[t], q_send.at[t], q_recv.at[t], z_peer[t]) for t in (1, 2)
    }
    own_copy = {
        t: remote(kv_own.at[0], kv_own.at[t], own_send.at[t], own_recv.at[t], z_peer[t])
        for t in (1, 2)
    }
    pairs = [w_pair(0)]

    partners = [partner_ref[0, seq], partner_ref[1, seq]]
    flips = [partner ^ seq for partner in partners]

    kv_b = [[], []]
    for kind in range(2):
        kv_a[kind, 2].wait_recv()
        kv_b[kind].append(kv_copy(kind, 3, 2, 3, 1))
        if kind == 0:
            kv_b[kind].append(kv_copy(kind, 4, 2, 4, 2))
        kv_a[kind, 6].wait_recv()
        kv_b[kind].append(kv_copy(kind, 5, 6, 5, 7))
        if kind == 1:
            kv_b[kind].append(kv_copy(kind, 4, 6, 4, 6))
    w_next(1)

    core_step = []
    for kind in range(2):
        pass_on([kv_a[kind, 1], kv_a[kind, 7], *kv_b[kind]])
        for i in range(2):
            by_core[kind][0, i] = by_y[kind][(y - (partners[i] >> 1)) & 7]
        core_step.append(remote(
            by_core[kind].at[0], by_core[kind].at[1],
            core_send.at[kind], core_recv.at[kind], other_core,
        ))
    z_step = {}
    for kind in range(2):
        core_step[kind].wait_recv()
        for i in range(2):
            kv_z[0, kind, i] = by_core[kind][flips[i] & 1, i]
        for t in (1, 2):
            z_step[t, kind] = remote(
                kv_z.at[0, kind], kv_z.at[t, kind],
                z_send.at[t, kind], z_recv.at[t, kind], z_peer[t],
            )

    w_next(2)
    w_next(3)
    for kind in range(2):
        z_step[2, kind].wait_recv()
        z_step[3, kind] = remote(
            kv_z.at[2, kind], kv_z.at[3, kind], z_send.at[3, kind], z_recv.at[3, kind], z_peer[1]
        )
    own_copy[2].wait_recv()
    own_copy[3] = remote(kv_own.at[2], kv_own.at[3], own_send.at[3], own_recv.at[3], z_peer[1])
    q_copy[2].wait_recv()
    q_copy[3] = remote(q_all.at[2], q_all.at[3], q_send.at[3], q_recv.at[3], z_peer[1])
    w_next(4)
    for t in (1, 3):
        for kind in range(2):
            z_step[t, kind].wait_recv()

    def places(fold, offset):
        return offset + jnp.where(
            offset < HALF, fold * HALF, (BLOCKS - 1 - fold) * HALF - HALF
        )

    down_iota = lax.broadcasted_iota(jnp.int32, (ROWS, ROWS), 0)
    across_iota = lax.broadcasted_iota(jnp.int32, (ROWS, ROWS), 1)
    scale = 1.0 / math.sqrt(DIM)

    def attend(t):
        if t % 2:
            q_copy[t].wait_recv()
            own_copy[t].wait_recv()
        device = seq ^ (16 * t)
        own_places = places(fold_ref[device], across_iota)
        hidden = []
        for source in (device, partner_ref[0, device], partner_ref[1, device]):
            seen = places(fold_ref[source], down_iota) <= own_places
            hidden.append(jnp.where(seen, 0.0, -jnp.inf).astype(jnp.float32))
        bias = jnp.concatenate(hidden, axis=0)
        bias = jnp.concatenate([bias] * 4, axis=1)
        slots = [t ^ ((flip >> 4) & 3) for flip in flips]
        keys = jnp.concatenate(
            [kv_own[t, keys_part, :]] + [kv_z[slots[i], 0, i] for i in range(2)], axis=0
        )
        values = jnp.concatenate(
            [kv_own[t, values_part, :]] + [kv_z[slots[i], 1, i] for i in range(2)], axis=1
        )
        for part in range(2):
            scores = dot_nt(keys, q_all[t, pl.ds(part * 4 * ROWS, 4 * ROWS), :]) * scale + bias
            top = jnp.max(scores, axis=0, keepdims=True)
            weights = jnp.exp(scores - top)
            total = jnp.sum(weights, axis=0, keepdims=True)
            summed = dot_nn(values, weights.astype(jnp.bfloat16)) / total
            summed = summed.astype(jnp.bfloat16)
            for h in range(4):
                att[t, pl.ds((part * 4 + h) * DIM, DIM), :] = summed[:, h * ROWS : (h + 1) * ROWS]

    attend(0)
    w_next(5)
    pass_on(pairs)

    x_copies = {}

    def product(t, quarter):
        rows = pl.ds(pl.multiple_of(quarter * QUARTER, 16), QUARTER)
        return dot_nn(w_all[rows, :], att[t])

    def project(t):
        for d in (2, 1, 3):
            x_out[t, d - 1] = product(t, quarter_of(x ^ d)).astype(jnp.bfloat16)
            x_copies[t, d] = remote(
                x_out.at[t, d - 1], x_in.at[t, d - 1],
                x_send.at[t, d - 1], x_recv.at[t, d - 1], x_peer[d],
            )
        kept[t] = product(t, own_quarter)

    slot_side = own_quarter % 2

    def last(t, hi, side):
        return pltpu.make_async_remote_copy(
            src_ref=s2_out.at[t], dst_ref=s2_in.at[hi, side],
            send_sem=s2_send.at[t], recv_sem=s2_recv.at[hi, side],
            device_id=targets[t], device_id_type=MESH,
        )

    def deliver(t):
        total = kept[t]
        for d in (1, 3, 2):
            x_copies[t, d].wait_recv()
            total = total + x_in[t, d - 1].astype(jnp.float32)
        s2_out[t] = total.astype(jnp.bfloat16)
        if t:
            last(t, z_hi, slot_side).start()
        else:
            pl.when(jnp.logical_not(home))(lambda: last(t, z_hi, slot_side).start())

            @pl.when(home)
            def _():
                pltpu.make_async_copy(
                    s2_out.at[t], s2_in.at[z_hi, slot_side], s2_recv.at[z_hi, slot_side]
                ).start()

    project(0)
    attend(1)
    project(1)
    attend(2)
    project(2)
    attend(3)
    project(3)
    deliver(0)
    deliver(1)
    deliver(2)
    deliver(3)

    for side in range(2):
        for hi in range(2):
            last(1, hi, side).wait_recv()
    for copy in sent:
        copy.wait_send()
    for t in range(1, 4):
        last(t, 0, 0).wait_send()

    @pl.when(jnp.logical_not(home))
    def _():
        last(0, 0, 0).wait_send()


def per_device(queries, key_heads, value_heads, fold_map, partner_map, out_weight):
    anywhere = pl.BlockSpec(memory_space=pl.ANY)
    smem = pl.BlockSpec(memory_space=pltpu.SMEM)
    bf16, f32 = jnp.bfloat16, jnp.float32
    dma = pltpu.SemaphoreType.DMA
    kv_rows = 2 * ROWS
    halves = pl.pallas_call(
        kernel,
        out_shape=jax.ShapeDtypeStruct((2, 2, QUARTER, ROWS), bf16),
        in_specs=[anywhere, anywhere, anywhere, smem, smem, anywhere],
        out_specs=anywhere,
        scratch_shapes=[
            pltpu.VMEM((DEPTH, DIM), bf16),
            pltpu.VMEM((ROWS, DIM), bf16),
            pltpu.VMEM((ROWS, DIM), bf16),
            pltpu.VMEM((DEPTH, DIM), f32),
            pltpu.VMEM((4, DEPTH, DIM), bf16),
            pltpu.VMEM((4, kv_rows, DIM), bf16),
            pltpu.VMEM((N_Y, ROWS, DIM), bf16),
            pltpu.VMEM((N_Y, ROWS, DIM), bf16),
            pltpu.VMEM((2, 2, ROWS, DIM), bf16),
            pltpu.VMEM((2, 2, ROWS, DIM), bf16),
            pltpu.VMEM((4, 2, 2, ROWS, DIM), bf16),
            pltpu.VMEM((16 * CHUNK, DEPTH), bf16),
            pltpu.VMEM((4, DEPTH, ROWS), bf16),
            pltpu.VMEM((4, QUARTER, ROWS), f32),
            pltpu.VMEM((4, 3, QUARTER, ROWS), bf16),
            pltpu.VMEM((4, 3, QUARTER, ROWS), bf16),
            pltpu.VMEM((4, QUARTER, ROWS), bf16),
            dma((4,)), dma((2, 8)), dma((2, 8)), dma((4, 2, 2)), dma((4, 2, 2)), dma((8,)), dma((8,)),
            dma((2,)), dma((2,)), dma((4,)), dma((4,)), dma((4,)), dma((4,)),
            dma((4, 2)), dma((4, 2)), dma((4, 3)), dma((4, 3)), dma((4,)), dma((2, 2)),
        ],
        compiler_params=pltpu.CompilerParams(
            collective_id=0, has_side_effects=True, vmem_limit_bytes=56 * 1024 * 1024
        ),
        cost_estimate=pl.CostEstimate(
            flops=1_550_000_000, bytes_accessed=1_000_000, transcendentals=400_000
        ),
    )(
        queries.reshape(ROWS * HEADS, DIM),
        key_heads.reshape(ROWS, DIM),
        value_heads.reshape(ROWS, DIM),
        fold_map,
        partner_map,
        out_weight.T,
    ).astype(f32)
    return (halves[0] + halves[1]).reshape(2 * QUARTER, ROWS).T.astype(bf16)


def solution(mesh):
    return jax.shard_map(
        per_device,
        mesh=mesh,
        in_specs=(
            P("seq", "head", None),
            P("seq", "head", None),
            P("seq", "head", None),
            P(),
            P(),
            P("head", "seq"),
        ),
        out_specs=P("seq", "head"),
        check_vma=False,
    )
```

```python
import math

import jax
import jax.numpy as jnp
from jax import lax
from jax.experimental import pallas as pl
from jax.experimental.pallas import tpu as pltpu
from jax.sharding import PartitionSpec as P

MESH = pl.DeviceIdType.MESH
HEADS = 8
DIM = 128
ROWS = 128
HALF = 64
DEPTH = HEADS * DIM
CHUNK = 80
QUARTER = 320
N_Y = 8
BLOCKS = 128


def dot_nt(a, b):
    return lax.dot_general(a, b, (((1,), (1,)), ((), ())), preferred_element_type=jnp.float32)


def dot_nn(a, b):
    return lax.dot_general(a, b, (((1,), (0,)), ((), ())), preferred_element_type=jnp.float32)


def kernel(
    q_hbm, k_hbm, v_hbm, fold_ref, partner_ref, w_hbm, s2_in,
    q_in, k_in, v_in, q_wide, q_all, kv_own, k_y, v_y, k_c, v_c, kv_z, w_all, att,
    kept, x_out, x_in, s2_out,
    in_sem, y_send, y_recv, w_send, w_recv, pair_send, pair_recv, core_send, core_recv,
    q_send, q_recv, own_send, own_recv, z_send, z_recv, x_send, x_recv, s2_send, s2_recv,
):
    seq = lax.axis_index("seq")
    head = lax.axis_index("head")
    z, y, core = seq // 16, (seq // 2) % 8, seq % 2
    z_hi, x = head // 4, head % 4

    def at(z_to, y_to, core_to):
        return z_to * 16 + y_to * 2 + core_to

    def w_rows(k):
        return pl.multiple_of((((y - k) % 8) * 2 + core) * CHUNK, 16)

    w_own = pl.ds(w_rows(0), CHUNK)
    loads = [
        pltpu.make_async_copy(src, dst, in_sem.at[i])
        for i, (src, dst) in enumerate(
            ((k_hbm, k_in), (v_hbm, v_in), (q_hbm, q_in), (w_hbm, w_all.at[w_own]))
        )
    ]
    for load in loads:
        load.start()

    y_peer = {k: (at(z, (y + k) % 8, core), head) for k in (1, 2, 6, 7)}
    z_peer = {t: (seq ^ (16 * t), head) for t in (1, 2, 3)}
    x_peer = {d: (seq, head ^ d) for d in (1, 2, 3)}
    other_core = (seq ^ 1, head)

    def quarter_of(owner):
        turned = (owner + 2 * (z % 2)) % 4
        return jnp.where(turned < 2, 2 * turned, 7 - 2 * turned)

    own_quarter = quarter_of(x)
    target_head = 2 * z + own_quarter // 2
    targets = [(seq ^ (16 * t), target_head) for t in range(4)]
    home = target_head == head
    source_seq = at(head // 2, y, core)

    barrier = pltpu.get_barrier_semaphore()
    peers = [*y_peer.values(), *z_peer.values(), *x_peer.values(), other_core]
    for peer in peers:
        pl.semaphore_signal(barrier, inc=1, device_id=peer, device_id_type=MESH)
    for hi in range(2):
        for side in range(2):
            source_x = (head % 2 if side == 0 else 3 - head % 2) + 2 * ((head // 2) % 2)
            source_head = hi * 4 + source_x % 4
            mine = jnp.logical_and(source_seq == seq, source_head == head)

            @pl.when(jnp.logical_not(mine))
            def _():
                pl.semaphore_signal(
                    barrier, inc=1, device_id=(source_seq, source_head), device_id_type=MESH
                )

    loads[0].wait()
    loads[1].wait()
    turned = jnp.transpose(v_in[...].astype(jnp.float32)).astype(jnp.bfloat16)
    kv_own[0, 0:ROWS, :] = k_in[...]
    kv_own[0, ROWS:, :] = turned
    k_y[0] = k_in[...]
    v_y[0] = turned
    loads[2].wait()
    q_wide[...] = q_in[...].astype(jnp.float32)
    for h in range(HEADS):
        q_all[0, pl.ds(h * ROWS, ROWS), :] = q_wide[
            pl.ds(h, ROWS, stride=HEADS), :
        ].astype(jnp.bfloat16)
    loads[3].wait()
    pl.semaphore_wait(barrier, len(peers) + 4 - jnp.where(home, 1, 0))

    sent = []

    def remote(src, dst, send, recv, peer):
        copy = pltpu.make_async_remote_copy(
            src_ref=src, dst_ref=dst, send_sem=send, recv_sem=recv,
            device_id=peer, device_id_type=MESH,
        )
        copy.start()
        sent.append(copy)
        return copy

    def pass_on(copies):
        for copy in copies:
            copy.wait_recv()

    keys_part, values_part = pl.ds(0, ROWS), pl.ds(ROWS, ROWS)
    by_y, by_core = (k_y, v_y), (k_c, v_c)

    def kv_copy(kind, i, from_slot, to_slot, peer):
        return remote(
            by_y[kind].at[from_slot], by_y[kind].at[to_slot],
            y_send.at[kind, i], y_recv.at[kind, i], y_peer[peer],
        )

    w_streams = ((0, 48), (48, CHUNK - 48))

    def w_hop(k, stream):
        first, rows = w_streams[stream]
        copies = []
        for way, slot, peer in ((0, k - 1, 1), (1, (9 - k) % 8, 7)):
            place = pl.ds(pl.multiple_of(w_rows(slot) + first, 16), rows)
            sem = (k - 1, way, stream)
            copies.append(remote(
                w_all.at[place], w_all.at[place], w_send.at[sem], w_recv.at[sem], y_peer[peer]
            ))
        if k == 3:
            slot = (2, 6)[stream]
            place = pl.ds(pl.multiple_of(w_rows(slot) + first, 16), rows)
            sem = (3, stream, 0)
            copies.append(remote(
                w_all.at[place], w_all.at[place], w_send.at[sem], w_recv.at[sem], y_peer[slot]
            ))
        return copies

    hops = {}

    def w_next(k):
        for stream in range(2):
            if k > 1:
                pass_on(hops[k - 1, stream])
            if k < 4:
                hops[k, stream] = w_hop(k, stream)
        for slot in {2: (1, 7), 3: (2, 6), 4: (3, 5, 4)}.get(k, ()):
            pairs.append(w_pair(slot))

    def w_pair(k):
        place = pl.ds(w_rows(k), CHUNK)
        return remote(w_all.at[place], w_all.at[place], pair_send.at[k], pair_recv.at[k], other_core)

    kv_a = {(kind, k): kv_copy(kind, k, 0, k, k) for kind in range(2) for k in (2, 6, 1, 7)}
    q_copy = {
        t: remote(q_all.at[0], q_all.at[t], q_send.at[t], q_recv.at[t], z_peer[t]) for t in (1, 2)
    }
    own_copy = {
        t: remote(kv_own.at[0], kv_own.at[t], own_send.at[t], own_recv.at[t], z_peer[t])
        for t in (1, 2)
    }
    pairs = [w_pair(0)]

    partners = [partner_ref[0, seq], partner_ref[1, seq]]
    flips = [partner ^ seq for partner in partners]

    kv_b = [[], []]
    for kind in range(2):
        kv_a[kind, 2].wait_recv()
        kv_b[kind].append(kv_copy(kind, 3, 2, 3, 1))
        if kind == 0:
            kv_b[kind].append(kv_copy(kind, 4, 2, 4, 2))
        kv_a[kind, 6].wait_recv()
        kv_b[kind].append(kv_copy(kind, 5, 6, 5, 7))
        if kind == 1:
            kv_b[kind].append(kv_copy(kind, 4, 6, 4, 6))
    w_next(1)

    core_step = []
    for kind in range(2):
        pass_on([kv_a[kind, 1], kv_a[kind, 7], *kv_b[kind]])
        for i in range(2):
            by_core[kind][0, i] = by_y[kind][(y - (partners[i] >> 1)) & 7]
        core_step.append(remote(
            by_core[kind].at[0], by_core[kind].at[1],
            core_send.at[kind], core_recv.at[kind], other_core,
        ))
    z_step = {}
    for kind in range(2):
        core_step[kind].wait_recv()
        for i in range(2):
            kv_z[0, kind, i] = by_core[kind][flips[i] & 1, i]
        for t in (1, 2):
            z_step[t, kind] = remote(
                kv_z.at[0, kind], kv_z.at[t, kind],
                z_send.at[t, kind], z_recv.at[t, kind], z_peer[t],
            )

    w_next(2)
    w_next(3)
    for kind in range(2):
        z_step[2, kind].wait_recv()
        z_step[3, kind] = remote(
            kv_z.at[2, kind], kv_z.at[3, kind], z_send.at[3, kind], z_recv.at[3, kind], z_peer[1]
        )
    own_copy[2].wait_recv()
    own_copy[3] = remote(kv_own.at[2], kv_own.at[3], own_send.at[3], own_recv.at[3], z_peer[1])
    q_copy[2].wait_recv()
    q_copy[3] = remote(q_all.at[2], q_all.at[3], q_send.at[3], q_recv.at[3], z_peer[1])
    w_next(4)
    for t in (1, 3):
        for kind in range(2):
            z_step[t, kind].wait_recv()

    def places(fold, offset):
        return offset + jnp.where(
            offset < HALF, fold * HALF, (BLOCKS - 1 - fold) * HALF - HALF
        )

    down_iota = lax.broadcasted_iota(jnp.int32, (ROWS, ROWS), 0)
    across_iota = lax.broadcasted_iota(jnp.int32, (ROWS, ROWS), 1)
    scale = 1.0 / math.sqrt(DIM)

    def attend(t):
        if t % 2:
            q_copy[t].wait_recv()
            own_copy[t].wait_recv()
        device = seq ^ (16 * t)
        own_places = places(fold_ref[device], across_iota)
        hidden = []
        for source in (device, partner_ref[0, device], partner_ref[1, device]):
            seen = places(fold_ref[source], down_iota) <= own_places
            hidden.append(jnp.where(seen, 0.0, -jnp.inf).astype(jnp.float32))
        bias = jnp.concatenate(hidden, axis=0)
        bias = jnp.concatenate([bias] * 4, axis=1)
        slots = [t ^ ((flip >> 4) & 3) for flip in flips]
        keys = jnp.concatenate(
            [kv_own[t, keys_part, :]] + [kv_z[slots[i], 0, i] for i in range(2)], axis=0
        )
        values = jnp.concatenate(
            [kv_own[t, values_part, :]] + [kv_z[slots[i], 1, i] for i in range(2)], axis=1
        )
        for part in range(2):
            scores = dot_nt(keys, q_all[t, pl.ds(part * 4 * ROWS, 4 * ROWS), :]) * scale + bias
            top = jnp.max(scores, axis=0, keepdims=True)
            weights = jnp.exp(scores - top)
            total = jnp.sum(weights, axis=0, keepdims=True)
            summed = dot_nn(values, weights.astype(jnp.bfloat16)) / total
            summed = summed.astype(jnp.bfloat16)
            for h in range(4):
                att[t, pl.ds((part * 4 + h) * DIM, DIM), :] = summed[:, h * ROWS : (h + 1) * ROWS]

    attend(0)
    pass_on(pairs)

    x_copies = {}

    def product(t, quarter):
        rows = pl.ds(pl.multiple_of(quarter * QUARTER, 16), QUARTER)
        return dot_nn(w_all[rows, :], att[t])

    def project(t):
        for d in (2, 1, 3):
            x_out[t, d - 1] = product(t, quarter_of(x ^ d)).astype(jnp.bfloat16)
            x_copies[t, d] = remote(
                x_out.at[t, d - 1], x_in.at[t, d - 1],
                x_send.at[t, d - 1], x_recv.at[t, d - 1], x_peer[d],
            )
        kept[t] = product(t, own_quarter)

    slot_side = own_quarter % 2

    def last(t, hi, side):
        return pltpu.make_async_remote_copy(
            src_ref=s2_out.at[t], dst_ref=s2_in.at[hi, side],
            send_sem=s2_send.at[t], recv_sem=s2_recv.at[hi, side],
            device_id=targets[t], device_id_type=MESH,
        )

    def deliver(t):
        total = kept[t]
        for d in (1, 3, 2):
            x_copies[t, d].wait_recv()
            total = total + x_in[t, d - 1].astype(jnp.float32)
        s2_out[t] = total.astype(jnp.bfloat16)
        if t:
            last(t, z_hi, slot_side).start()
        else:
            pl.when(jnp.logical_not(home))(lambda: last(t, z_hi, slot_side).start())

            @pl.when(home)
            def _():
                pltpu.make_async_copy(
                    s2_out.at[t], s2_in.at[z_hi, slot_side], s2_recv.at[z_hi, slot_side]
                ).start()

    project(0)
    attend(1)
    project(1)
    attend(2)
    project(2)
    attend(3)
    project(3)
    deliver(0)
    deliver(1)
    deliver(2)
    deliver(3)

    for side in range(2):
        for hi in range(2):
            last(1, hi, side).wait_recv()
    for copy in sent:
        copy.wait_send()
    for t in range(1, 4):
        last(t, 0, 0).wait_send()

    @pl.when(jnp.logical_not(home))
    def _():
        last(0, 0, 0).wait_send()


def per_device(queries, key_heads, value_heads, fold_map, partner_map, out_weight):
    anywhere = pl.BlockSpec(memory_space=pl.ANY)
    smem = pl.BlockSpec(memory_space=pltpu.SMEM)
    bf16, f32 = jnp.bfloat16, jnp.float32
    dma = pltpu.SemaphoreType.DMA
    kv_rows = 2 * ROWS
    halves = pl.pallas_call(
        kernel,
        out_shape=jax.ShapeDtypeStruct((2, 2, QUARTER, ROWS), bf16),
        in_specs=[anywhere, anywhere, anywhere, smem, smem, anywhere],
        out_specs=anywhere,
        scratch_shapes=[
            pltpu.VMEM((DEPTH, DIM), bf16),
            pltpu.VMEM((ROWS, DIM), bf16),
            pltpu.VMEM((ROWS, DIM), bf16),
            pltpu.VMEM((DEPTH, DIM), f32),
            pltpu.VMEM((4, DEPTH, DIM), bf16),
            pltpu.VMEM((4, kv_rows, DIM), bf16),
            pltpu.VMEM((N_Y, ROWS, DIM), bf16),
            pltpu.VMEM((N_Y, ROWS, DIM), bf16),
            pltpu.VMEM((2, 2, ROWS, DIM), bf16),
            pltpu.VMEM((2, 2, ROWS, DIM), bf16),
            pltpu.VMEM((4, 2, 2, ROWS, DIM), bf16),
            pltpu.VMEM((16 * CHUNK, DEPTH), bf16),
            pltpu.VMEM((4, DEPTH, ROWS), bf16),
            pltpu.VMEM((4, QUARTER, ROWS), f32),
            pltpu.VMEM((4, 3, QUARTER, ROWS), bf16),
            pltpu.VMEM((4, 3, QUARTER, ROWS), bf16),
            pltpu.VMEM((4, QUARTER, ROWS), bf16),
            dma((4,)), dma((2, 8)), dma((2, 8)), dma((4, 2, 2)), dma((4, 2, 2)), dma((8,)), dma((8,)),
            dma((2,)), dma((2,)), dma((4,)), dma((4,)), dma((4,)), dma((4,)),
            dma((4, 2)), dma((4, 2)), dma((4, 3)), dma((4, 3)), dma((4,)), dma((2, 2)),
        ],
        compiler_params=pltpu.CompilerParams(
            collective_id=0, has_side_effects=True, vmem_limit_bytes=56 * 1024 * 1024
        ),
        cost_estimate=pl.CostEstimate(
            flops=1_550_000_000, bytes_accessed=1_000_000, transcendentals=400_000
        ),
    )(
        queries.reshape(ROWS * HEADS, DIM),
        key_heads.reshape(ROWS, DIM),
        value_heads.reshape(ROWS, DIM),
        fold_map,
        partner_map,
        out_weight.T,
    ).astype(f32)
    return (halves[0] + halves[1]).reshape(2 * QUARTER, ROWS).T.astype(bf16)


def solution(mesh):
    return jax.shard_map(
        per_device,
        mesh=mesh,
        in_specs=(
            P("seq", "head", None),
            P("seq", "head", None),
            P("seq", "head", None),
            P(),
            P(),
            P("head", "seq"),
        ),
        out_specs=P("seq", "head"),
        check_vma=False,
    )
```
